512 devices in a mesh: tm: 64 (over z, y), rows: 8 (over x, core).
Axes of the slice: x: 4, y: 4, z: 16, core: 2. Of those that a mesh axis runs over, the one named last changes fastest.
Arguments:
- features: bfloat16 [256, 224, 16, 256], P('tm', 'rows'), as said below
- clip_ids: int32 [256], P('tm'), may hold values from 0 to 63, as said below
- frame_valid: int32 [256], P('tm'), may hold values from 0 to 1, as said below
- norm_gain: float32 [256], replicated, may hold values from 0.1 to 1.9
- norm_bias: float32 [256], replicated, may hold values from -3 to 3
- conv_weight: bfloat16 [3, 3, 3, 256, 256], P(None, None, None, 'rows'), may hold values from -0.078125 to 0.078125
- down_weight: bfloat16 [3, 3, 256, 256], P(None, None, 'rows'), may hold values from -0.125 to 0.125
Outputs:
- reduced: bfloat16 [256, 112, 8, 256], P('tm', 'rows')
The draws below stay inside these ranges and needn't reach their ends.
Inputs may be any that keep to these rules, and one draw needn't show every extreme that they name: `clip_ids`: each of the 64 clips holds 2 to 6 consecutive frames, one exactly 6; the index never falls along time. `frame_valid`: a padding frame is the last frame of its clip, never its first. `features`: activations.
All inputs are finite; a program needn't handle non-finite values.
Results may differ from the reference program's by a relative error of at most 0.0051.
Values may be sent and summed in bfloat16 or wider, within the bound.
No kernel may reach another device: no remote copies, remote signals or barrier semaphores. Data moves between devices by JAX's collectives and lax.ppermute only.
A program may use at most 64 MiB of HBM per device.

```python
import jax
import jax.numpy as jnp
from jax import lax

C = 256
GROUPS = 32
COLS = 16
NT = 256
ROWS = 224
NCLIPS = 64


def draw_features(key, part):
    key = jax.random.fold_in(key, 11)
    key_frame, key_row, key_noise, key_ramp, key_col, key_scale = jax.random.split(key, 6)
    times = jnp.arange(NT, dtype=jnp.float32)
    scale = 0.5 + times / max(NT - 1, 1)
    group_off = jax.random.normal(key_frame, (NT, 1, 1, GROUPS), jnp.float32)
    frame_off = jnp.repeat(group_off, C // GROUPS, axis=3)
    row_off = jax.random.normal(key_row, (1, ROWS, 1, C), jnp.float32) * 0.7
    ramp_amp = jax.random.normal(key_ramp, (1, 1, 1, GROUPS), jnp.float32) * 0.8
    ramp_amp = jnp.repeat(ramp_amp, C // GROUPS, axis=3)
    ramp_rows = 2.0 * jnp.arange(ROWS, dtype=jnp.float32) / max(ROWS - 1, 1) - 1.0
    ramp = ramp_amp * ramp_rows[None, :, None, None]
    column_group = jax.random.normal(key_col, (1, 1, COLS, GROUPS), jnp.float32) * 0.6
    column_off = jnp.repeat(column_group, C // GROUPS, axis=3)
    column_scale = jnp.exp(jax.random.uniform(key_scale, (1, 1, COLS, 1), jnp.float32, -0.9, 0.9))
    noise = jax.random.normal(key_noise, (NT, ROWS, COLS, C), jnp.float32)
    values = (frame_off + row_off + ramp + column_off + noise * column_scale) * scale[:, None, None, None]
    return values.astype(jnp.bfloat16)


def clip_starts(key):
    key = jax.random.fold_in(key, 5)
    key_kind, key_pick = jax.random.split(key, 2)
    pair_count = NCLIPS // 2
    kinds = jax.random.randint(key_kind, (pair_count,), 0, 8, dtype=jnp.int32)
    chosen = jax.random.randint(key_pick, (), 0, pair_count - 1, dtype=jnp.int32)
    pair_at = jnp.arange(pair_count, dtype=jnp.int32)
    kinds = jnp.where(pair_at == chosen, 0, kinds)
    firsts = jnp.where(kinds < 4, 6, kinds - 2).astype(jnp.int32)
    places = jnp.arange(NCLIPS, dtype=jnp.int32)
    pair_of = jnp.clip((places - 1) // 2, 0, pair_count - 1)
    second = (places - 1) % 2 == 1
    picked = firsts[pair_of]
    lengths = jnp.where(second, 8 - picked, picked)
    lengths = jnp.where(places == 0, 3, lengths)
    lengths = jnp.where(places == NCLIPS - 1, 5, lengths).astype(jnp.int32)
    starts = (jnp.cumsum(lengths) - lengths).astype(jnp.int32)
    in_chosen = jnp.logical_and(places >= 1, pair_of == chosen)
    kept = jnp.logical_and(in_chosen, jnp.logical_not(second))
    forced = jnp.logical_and(in_chosen, second)
    return (starts, lengths, kept, forced)


def draw_clip_ids(key, part):
    starts, lengths, kept, forced = clip_starts(key)
    frames_at = jnp.arange(NT, dtype=jnp.int32)
    later = (frames_at[:, None] >= starts[None, 1:]).astype(jnp.int32)
    return jnp.sum(later, axis=1).astype(jnp.int32)


def draw_frame_valid(key, part):
    starts, lengths, kept, forced = clip_starts(key)
    key = jax.random.fold_in(key, 13)
    coins = jax.random.randint(key, (NCLIPS,), 0, 2, dtype=jnp.int32)
    ends = starts + lengths
    dropped = jnp.logical_and(lengths >= 2, coins == 1)
    dropped = jnp.logical_and(dropped, jnp.logical_not(kept))
    dropped = jnp.logical_or(dropped, forced)
    frames_at = jnp.arange(NT, dtype=jnp.int32)
    hits = jnp.logical_and(frames_at[:, None] == (ends - 1)[None, :], dropped[None, :]).astype(jnp.int32)
    return (1 - jnp.sum(hits, axis=1)).astype(jnp.int32)


def steps_of(rng, extent, shards, least, largest):
    gain, own = 1.0, jax.random.fold_in(rng, 6)
    for axis_at, blocks in shards:
        heights = jnp.exp(jax.random.uniform(jax.random.fold_in(own, axis_at), (blocks,), jnp.float32, least / len(shards), largest / len(shards)))
        gain = gain * jnp.repeat(heights, extent[axis_at] // blocks).reshape([-1 if axis == axis_at else 1 for axis in range(len(extent))])
    return gain


def scatter_about(stream_key, shape, width, most, shards=(), kind=jnp.bfloat16):
    array = width * jax.random.normal(stream_key, shape, jnp.float32)
    if shards:
        array = array * steps_of(stream_key, shape, shards, -0.22, 0.18)
    return jnp.clip(array, -most, most).astype(kind)


def setup_inputs(seed: int = 0) -> dict:
    streams_of = jax.random.split(jax.random.key(seed), 8)
    features = draw_features(jax.random.fold_in(streams_of[7], 71), 0)
    clip_ids = draw_clip_ids(jax.random.fold_in(streams_of[7], 71), 0)
    frame_valid = draw_frame_valid(jax.random.fold_in(streams_of[7], 71), 0)
    norm_gain = jnp.clip(1.0 + 0.18 * jax.random.normal(streams_of[3], (C,), jnp.float32), 0.1, 1.9)
    norm_bias = scatter_about(streams_of[4], (C,), 0.5, 3.0, (), jnp.float32)
    conv_weight = scatter_about(streams_of[5], (3, 3, 3, C, C), (27 * C) ** -0.5, 0.078125, ((3, 8),))
    down_weight = scatter_about(streams_of[6], (3, 3, C, C), (9 * C) ** -0.5, 0.125, ((2, 8),))
    return dict(features=features, clip_ids=clip_ids, frame_valid=frame_valid, norm_gain=norm_gain, norm_bias=norm_bias, conv_weight=conv_weight, down_weight=down_weight)


def activate(block, mean_val, inv_std, frame_weight, gain_vec, bias_vec):
    frames, height, across, channels = block.shape
    groups = mean_val.shape[1]
    grouped = block.astype(jnp.float32).reshape(frames, height, across, groups, channels // groups)
    scaled = (grouped - mean_val[:, None, None, :, None]) * inv_std[:, None, None, :, None]
    scaled = scaled.reshape(frames, height, across, channels) * gain_vec + bias_vec
    return (jax.nn.silu(scaled) * frame_weight[:, None, None, None]).astype(jnp.bfloat16)

def local_stats(block, valid_f, groups):
    frames, height, across, channels = block.shape
    grouped = block.astype(jnp.float32).reshape(frames, height * across, groups, channels // groups)
    first_sum = lax.optimization_barrier(jnp.sum(grouped, axis=(1, 3)))
    square_sum = lax.optimization_barrier(jnp.sum(grouped * grouped, axis=(1, 3)))
    sums = jnp.stack([first_sum, square_sum], axis=-1) * valid_f[:, None, None]
    counts = valid_f * float(height * across * (channels // groups))
    return (sums, counts)

def finish_stats(sums_fg, counts_f):
    safe = jnp.maximum(counts_f, 1.0)[:, None]
    mean_val = sums_fg[..., 0] / safe
    spread = jnp.maximum(sums_fg[..., 1] / safe - mean_val * mean_val, 0.0)
    return (mean_val, lax.rsqrt(spread + 1e-05))

def conv_part(columns, masks, weight_piece):
    frames = masks.shape[1]
    height = columns.shape[1] - 2
    channels = weight_piece.shape[3]
    width_out = weight_piece.shape[4]
    total = jnp.zeros((frames, height, columns.shape[2], width_out), jnp.float32)
    for tap_time in range(3):
        partial_sum = jnp.zeros_like(total)
        for tap_row in range(3):
            patch = columns[tap_time:tap_time + frames, tap_row:tap_row + height]
            kernel = weight_piece[tap_time, tap_row].reshape(3 * channels, width_out)
            partial_sum = partial_sum + jnp.einsum('frwc,cn->frwn', patch, kernel, preferred_element_type=jnp.float32)
        total = total + masks[tap_time][:, None, None, None] * partial_sum
    return total

def down_part(dcolumns, weight_piece):
    height_out = (dcolumns.shape[1] - 1) // 2
    channels = weight_piece.shape[2]
    width_out = weight_piece.shape[3]
    total = jnp.zeros((dcolumns.shape[0], height_out, dcolumns.shape[2], width_out), jnp.float32)
    for tap_row in range(3):
        patch = dcolumns[:, tap_row:tap_row + 2 * height_out - 1:2]
        kernel = weight_piece[tap_row].reshape(3 * channels, width_out)
        total = total + jnp.einsum('frwc,cn->frwn', patch, kernel, preferred_element_type=jnp.float32)
    return total

def reference(features, clip_ids, frame_valid, norm_gain, norm_bias, conv_weight, down_weight):
    valid_f = frame_valid.astype(jnp.float32)
    sums, counts = local_stats(features, valid_f, GROUPS)
    onehot = (clip_ids[:, None] == jnp.arange(NCLIPS, dtype=jnp.int32)[None, :]).astype(jnp.float32)
    table_s = jnp.einsum('fc,fgk->cgk', onehot, sums, precision=lax.Precision.HIGHEST)
    table_n = jnp.dot(counts, onehot, precision=lax.Precision.HIGHEST)
    frame_s = jnp.einsum('fc,cgk->fgk', onehot, table_s, precision=lax.Precision.HIGHEST)
    frame_n = jnp.dot(onehot, table_n, precision=lax.Precision.HIGHEST)
    mean_val, inv_std = finish_stats(frame_s, frame_n)
    normed = activate(features, mean_val, inv_std, valid_f, norm_gain, norm_bias)
    h_padded = jnp.concatenate([jnp.zeros((2,) + normed.shape[1:], jnp.bfloat16), normed], axis=0)
    ids_padded = jnp.concatenate([jnp.full((2,), -1, jnp.int32), clip_ids.astype(jnp.int32)])

    def one_frame(index):
        block = lax.dynamic_slice_in_dim(h_padded, index, 3, 0)
        ids_three = lax.dynamic_slice_in_dim(ids_padded, index, 3, 0)
        masks = (ids_three == ids_three[2]).astype(jnp.float32)[:, None]
        padded = jnp.pad(block, ((0, 0), (1, 1), (1, 1), (0, 0)))
        columns = jnp.concatenate([padded[:, :, tap:tap + COLS] for tap in range(3)], axis=-1)
        conv = conv_part(columns, masks, conv_weight)
        x_frame = lax.dynamic_slice_in_dim(features, index, 1, 0).astype(jnp.float32)
        valid_one = lax.dynamic_slice_in_dim(valid_f, index, 1, 0)
        mixed = (valid_one[:, None, None, None] * (x_frame + conv)).astype(jnp.bfloat16)
        extended = jnp.pad(mixed, ((0, 0), (0, 1), (0, 1), (0, 0)))
        dcolumns = jnp.concatenate([extended[:, :, tap:tap + COLS - 1:2] for tap in range(3)], axis=-1)
        return down_part(dcolumns, down_weight).astype(jnp.bfloat16)[0]
    return lax.map(one_frame, jnp.arange(NT, dtype=jnp.int32))
```

```python
import jax
import jax.numpy as jnp
from jax import lax
from jax.experimental import pallas as pl
from jax.experimental.pallas import tpu as pltpu
from jax.sharding import PartitionSpec as P

GROUPS = 32
ID_LANE = 64
VALID_LANE = 65
BLOCK = 4
F32 = jnp.float32
BF16 = jnp.bfloat16


def shifted(value, axis, steps):
    count = lax.axis_size(axis)
    first, last = (max(0, -steps), min(count, count - steps))
    return lax.ppermute(value, axis, [(source, source + steps) for source in range(first, last)])


def swapped(value, axis, bits):
    return lax.ppermute(value, axis, [(i, i ^ bits) for i in range(lax.axis_size(axis))])


def ring_move(value, axis, cross):
    chips = lax.axis_size(axis) // 2
    pairs = []
    for chip in range(chips):
        for core in range(2):
            source_chip = (chip + (-1 if core == 0 else 1)) % chips
            pairs.append((2 * source_chip + (core ^ cross), 2 * chip + core))
    return lax.ppermute(value, axis, pairs)


def group_lanes(channels, first):
    lane = lax.broadcasted_iota(jnp.int32, (channels, 128), 1)
    group = lax.broadcasted_iota(jnp.int32, (channels, 128), 0) // (channels // GROUPS) + first
    return (lane == group).astype(F32)


def exact_dot(lhs, rhs):
    return lax.dot_general(
        lhs,
        rhs,
        (((1,), (0,)), ((), ())),
        precision=lax.Precision.HIGHEST,
        preferred_element_type=F32,
    )


def pack_kernel(
    place, ids, valid, feat, plain, gain, bias, cross, swap, table, params, kept
):
    frames, height, across, channels = feat.shape
    taps, slice_in, _ = plain.shape
    for message in (cross, swap):
        message[0:taps] = plain[...]
    for core in range(2):

        @pl.when(place[0] % 2 == core)
        def _(core=core):
            first_rows = feat[:, 0:2].reshape(frames, slice_in, channels)
            last_rows = feat[:, height - 2 :].reshape(frames, slice_in, channels)
            cross[taps:] = last_rows if core else first_rows
            swap[taps:] = first_rows if core else last_rows

    kept[...] = feat[...]
    params[0:1, :] = gain[...]
    params[1:2, :] = bias[...]

    first, second = [], []
    for f in range(frames):
        block = feat[f].astype(F32).reshape(height * across, channels)
        first.append(jnp.sum(block, axis=0, keepdims=True))
        second.append(jnp.sum(block * block, axis=0, keepdims=True))
    rows = exact_dot(
        jnp.concatenate(first + first, axis=0), group_lanes(channels, 0)
    ) + exact_dot(jnp.concatenate(second + second, axis=0), group_lanes(channels, GROUPS))
    lane = lax.broadcasted_iota(jnp.int32, (1, 128), 1)
    for at in range(2 * frames):
        weight = valid[at % frames].astype(F32)
        row = rows[at : at + 1, :] * weight
        row = jnp.where(lane == ID_LANE, ids[at % frames].astype(F32) + 1.0, row)
        table[at : at + 1, :] = jnp.where(lane == VALID_LANE, weight, row)


def pack_call(place, clip_ids, frame_valid, features, plain, gain, bias):
    frames, channels = features.shape[0], features.shape[-1]
    taps, slice_in, _ = plain.shape
    vmem = pl.BlockSpec(memory_space=pltpu.VMEM)
    return pl.pallas_call(
        pack_kernel,
        out_shape=(
            jax.ShapeDtypeStruct((taps + frames, slice_in, channels), BF16),
            jax.ShapeDtypeStruct((taps + frames, slice_in, channels), BF16),
            jax.ShapeDtypeStruct((2 * frames, 128), F32),
            jax.ShapeDtypeStruct((8, channels), F32),
            jax.ShapeDtypeStruct(features.shape, BF16),
        ),
        in_specs=[pl.BlockSpec(memory_space=pltpu.SMEM)] * 3 + [vmem] * 4,
        out_specs=(vmem,) * 5,
        compiler_params=pltpu.CompilerParams(vmem_limit_bytes=24 << 20),
        name="pack_and_sum",
    )(place, clip_ids, frame_valid, features, plain, gain, bias)


def halo_kernel(place, cross, swap, feat, out):
    frames, height, across, channels = feat.shape
    taps = cross.shape[0] - frames
    out[:, 1 : height + 1] = feat[frames - 2 :]
    for core in range(2):

        @pl.when(place[0] % 2 == core)
        def _(core=core):
            above, below = (swap, cross) if core else (cross, swap)
            rows = above[taps + frames - 2 :].reshape(2, 2, across, channels)
            out[:, 0:1] = rows[:, 1:2]
            out[:, height + 1 :] = below[taps + frames - 2 :].reshape(2, 2, across, channels)


def halo_call(place, cross, swap, feat):
    frames, height, across, channels = feat.shape
    vmem = pl.BlockSpec(memory_space=pltpu.VMEM)
    return pl.pallas_call(
        halo_kernel,
        out_shape=jax.ShapeDtypeStruct((2, height + 3, across, channels), BF16),
        in_specs=[pl.BlockSpec(memory_space=pltpu.SMEM)] + [vmem] * 3,
        out_specs=vmem,
        compiler_params=pltpu.CompilerParams(vmem_limit_bytes=16 << 20),
        name="halo",
    )(place, cross, swap, feat)


def held_places(band):
    chip, core = band // 2, band % 2
    near_chip = (chip + 3 + 2 * core) % 4
    far_chip = (chip + 2) % 4
    return [band, 2 * near_chip + core, 2 * near_chip + 1 - core, 2 * far_chip + core]


def main_kernel(place, block, params, feat, prev, *rest):
    pieces, (out, w_all, hcol, mixed_all, top, bottom, sems) = rest[:8], rest[8:]
    frames, height, across, channels = feat.shape
    taps, slice_in = pieces[0].shape[:2]
    taps_conv = 27

    band = place[0]
    places = held_places(band) + held_places(band + 1 - 2 * (band % 2))
    copies = []
    for at in range(8):
        start = pl.multiple_of(places[at] * slice_in, slice_in)
        source, target = pieces[at].at[0:taps], w_all.at[:, pl.ds(start, slice_in), :]
        copies.append(pltpu.make_async_copy(source, target, sems.at[at]))
    for copy in copies:
        copy.start()

    cross, swap = pieces[2], pieces[4]
    for core in range(2):

        @pl.when(band % 2 == core)
        def _(core=core):
            above, below = (swap, cross) if core else (cross, swap)
            top[...] = above[taps:].reshape(frames, 2, across, channels)[:, 1:2]
            bottom[...] = below[taps:].reshape(frames, 2, across, channels)

    bands = block.shape[1]
    here = place[1] % BLOCK

    def lane_of(rows, at):
        lane = lax.broadcasted_iota(jnp.int32, rows.shape, 1)
        return jnp.sum(jnp.where(lane == at, rows, 0.0), axis=1, keepdims=True)

    own_rows = block[here, 0]
    own_ids = lane_of(own_rows, ID_LANE)
    own_valid = lane_of(own_rows, VALID_LANE)
    total = jnp.zeros((8, 128), F32)
    for device in range(BLOCK):
        table = block[device, 0]
        table_ids = lane_of(table, ID_LANE)
        for sender in range(1, bands):
            table = table + block[device, sender]
        for f in range(2 * frames):
            same = table_ids[f : f + 1] == own_ids
            total = total + jnp.where(same, table[f : f + 1, :], 0.0)
    group = channels // GROUPS
    count = lane_of(total, VALID_LANE) * float(height * across * group)
    safe = jnp.maximum(count, 1.0)
    both = total / safe
    lane_at = lax.broadcasted_iota(jnp.int32, (128, channels), 0)
    group_at = lax.broadcasted_iota(jnp.int32, (128, channels), 1) // group
    mean = exact_dot(both, (lane_at == group_at).astype(F32))
    square = exact_dot(both, (lane_at == group_at + GROUPS).astype(F32))
    variance = jnp.maximum(square - mean * mean, 0.0)
    half_scale = 0.5 * (lax.rsqrt(variance + 1e-05) * params[0:1, :])
    half_bias = 0.5 * params[1:2, :]

    before_own = block[jnp.maximum(here - 1, 0), 0][frames - 2 : frames]
    before_sent = block[BLOCK - 1, 0][2 * frames - 2 : 2 * frames]
    before_rows = jnp.where(here > 0, before_own, before_sent)
    before_ids = lane_of(before_rows, ID_LANE)
    before_valid = lane_of(before_rows, VALID_LANE)

    top_ok = (band > 0).astype(F32)
    bottom_ok = (band < bands - 1).astype(F32)

    def normalise(x, at, weight, j, first, inside=None):
        rows = x.shape[0]
        x = x.astype(F32).reshape(rows * across, channels)
        u = (x - mean[at : at + 1]) * half_scale[at : at + 1] + half_bias
        h = (u + u * jnp.tanh(u)) * weight
        if inside is not None:
            h = jnp.where(jnp.full(h.shape, inside) > 0.0, h, 0.0)
        column = lax.broadcasted_iota(jnp.int32, h.shape, 0) % across
        left = jnp.where(column == 0, 0.0, pltpu.roll(h, 1, 0))
        right = jnp.where(column == across - 1, 0.0, pltpu.roll(h, rows * across - 1, 0))
        shape = (rows, across, channels)
        hcol[j, pl.ds(first, rows), :, 0:channels] = left.astype(BF16).reshape(shape)
        hcol[j, pl.ds(first, rows), :, channels : 2 * channels] = h.astype(BF16).reshape(shape)
        hcol[j, pl.ds(first, rows), :, 2 * channels :] = right.astype(BF16).reshape(shape)

    rows_step = 4
    for j in range(frames + 2):
        at = max(j - 2, 0)
        if j < 2:
            weight = before_valid[j : j + 1]
            source, source_at, shift = prev, j, 1
            normalise(prev[j, 0:1], at, weight, j, 0, top_ok)
            normalise(prev[j, height + 1 :], at, weight, j, height + 1, bottom_ok)
        else:
            weight = own_valid[at : at + 1]
            source, source_at, shift = feat, at, 0
            normalise(top[at], at, weight, j, 0, top_ok)
            normalise(bottom[at], at, weight, j, height + 1, bottom_ok)

        @pl.loop(0, height // rows_step)
        def _(step):
            first = step * rows_step
            x = source[source_at, pl.ds(first + shift, rows_step)]
            normalise(x, at, weight, j, first + 1)

    for copy in copies:
        copy.wait()

    out_rows = height + 1
    lane_parts = channels // 128
    ids_all = [before_ids[f : f + 1] for f in range(2)]
    ids_all = ids_all + [own_ids[f : f + 1] for f in range(frames)]
    for t in range(frames):
        total = None
        for dt in (2, 1, 0):
            part = None
            for dr in range(3):
                lhs = hcol[t + dt, dr : dr + out_rows].reshape(out_rows * across, 3 * channels)
                tap = (dt * 3 + dr) * 3
                rhs = w_all[tap : tap + 3].reshape(3 * channels, channels)
                product = jnp.dot(lhs, rhs, preferred_element_type=F32)
                part = product if part is None else part + product
            if dt == 2:
                total = part
            else:
                total = total + jnp.where(ids_all[t + dt] == ids_all[t + 2], part, 0.0)
        weight = own_valid[t : t + 1]
        body_rows = height * across
        main_rows = feat[t].astype(F32).reshape(body_rows, channels) + total[:body_rows]
        main_rows = (weight * main_rows).astype(BF16).astype(F32)
        main_rows = main_rows.reshape(height // 2, 2, across, channels)
        last_row = bottom[t, 0].astype(F32) + total[body_rows:]
        last_row = (weight * last_row * bottom_ok).astype(BF16).astype(F32)
        for part_at in range(lane_parts):
            lanes = slice(part_at * 128, (part_at + 1) * 128)
            mixed_all[part_at, t, 0 : height // 2] = main_rows[..., lanes]
            mixed_all[part_at, t, height // 2, 0] = last_row[:, lanes]

    half_rows, half_across = height // 2, across // 2
    points = frames * half_rows * half_across
    reduced = None
    for dr in range(3):
        rows_at, parity = (1 if dr == 2 else 0), dr % 2

        def every_second(first):
            columns = pl.ds(first, half_across, 2)
            return jnp.concatenate(
                [
                    mixed_all[at, :, rows_at : rows_at + half_rows, parity, columns, :].reshape(
                        points, 128
                    )
                    for at in range(lane_parts)
                ],
                axis=-1,
            )

        even, odd = every_second(0), every_second(1)
        column = lax.broadcasted_iota(jnp.int32, even.shape, 0) % half_across
        following = jnp.where(column == half_across - 1, 0.0, pltpu.roll(even, points - 1, 0))
        lhs = jnp.concatenate([even, odd, following], axis=-1).astype(BF16)
        tap = taps_conv + dr * 3
        rhs = w_all[tap : tap + 3].reshape(3 * channels, channels)
        product = jnp.dot(lhs, rhs, preferred_element_type=F32)
        reduced = product if reduced is None else reduced + product
    out[...] = reduced.astype(BF16)


def main_call(place, block, params, feat, prev, pieces):
    frames, height, across, channels = feat.shape
    taps = pieces[0].shape[0]
    points = frames * (height // 2) * (across // 2)
    vmem = pl.BlockSpec(memory_space=pltpu.VMEM)
    return pl.pallas_call(
        main_kernel,
        out_shape=jax.ShapeDtypeStruct((points, channels), BF16),
        in_specs=[pl.BlockSpec(memory_space=pltpu.SMEM)]
        + [vmem] * 12,
        out_specs=vmem,
        scratch_shapes=[
            pltpu.VMEM((taps, channels, channels), BF16),
            pltpu.VMEM((frames + 2, height + 3, across, 3 * channels), BF16),
            pltpu.VMEM((channels // 128, frames, height // 2 + 1, 2, across, 128), F32),
            pltpu.VMEM((frames, 1, across, channels), BF16),
            pltpu.VMEM((frames, 2, across, channels), BF16),
            pltpu.SemaphoreType.DMA((8,)),
        ],
        compiler_params=pltpu.CompilerParams(vmem_limit_bytes=28 << 20),
        name="norm_conv_down",
    )(place, block, params, feat, prev, *pieces)


def body(features, clip_ids, frame_valid, norm_gain, norm_bias, conv_weight, down_weight):
    frames, height, across, channels = features.shape
    slice_in = conv_weight.shape[3]
    place = jnp.stack([lax.axis_index("rows"), lax.axis_index("tm")]).astype(jnp.int32)

    bands, times = lax.axis_size("rows"), lax.axis_size("tm")

    plain = jnp.concatenate(
        [
            conv_weight.reshape(27, slice_in, channels),
            down_weight.reshape(9, slice_in, channels),
        ],
        axis=0,
    )
    cross, swap, table, params, feat = pack_call(
        place,
        clip_ids,
        frame_valid,
        features,
        plain,
        norm_gain.reshape(1, channels),
        norm_bias.reshape(1, channels),
    )

    near = ring_move(plain, "rows", 0)
    near_cross = ring_move(cross, "rows", 1)
    other = swapped(swap, "rows", 1)

    half = BLOCK // 2
    pairs = [(at, at + (BLOCK if at % BLOCK >= half else -BLOCK)) for at in range(times)]
    sent = lax.ppermute(table, "tm", [pair for pair in pairs if 0 <= pair[1] < times])
    row = lax.broadcasted_iota(jnp.int32, table.shape, 0)
    rows = jnp.where(row < frames, table, sent)
    size = BLOCK * bands
    groups = [[first + at for at in range(size)] for first in range(0, bands * times, size)]
    block = lax.all_to_all(
        jnp.broadcast_to(rows[None], (size, *rows.shape)),
        ("tm", "rows"),
        0,
        0,
        axis_index_groups=groups,
        tiled=True,
    ).reshape(BLOCK, bands, *rows.shape)

    near, near_cross, other, block = lax.optimization_barrier((near, near_cross, other, block))
    far = ring_move(near, "rows", 0)
    prev = shifted(halo_call(place, near_cross, other, feat), "tm", 1)
    far, prev = lax.optimization_barrier((far, prev))
    pieces = [plain, near, near_cross, far, other]
    pieces = pieces + [swapped(piece, "rows", 1) for piece in (near, near_cross, far)]

    out = main_call(place, block, params, feat, prev, pieces)
    return out.reshape(frames, height // 2, across // 2, channels)


def solution(mesh):
    return jax.shard_map(
        body,
        mesh=mesh,
        in_specs=(
            P("tm", "rows", None, None),
            P("tm"),
            P("tm"),
            P(),
            P(),
            P(None, None, None, "rows", None),
            P(None, None, "rows", None),
        ),
        out_specs=P("tm", "rows", None, None),
        check_vma=False,
    )
```

```python
import jax
import jax.numpy as jnp
from jax import lax
from jax.experimental import pallas as pl
from jax.experimental.pallas import tpu as pltpu
from jax.sharding import PartitionSpec as P

GROUPS = 32
ID_LANE = 64
VALID_LANE = 65
BLOCK = 4
F32 = jnp.float32
BF16 = jnp.bfloat16


def shifted(value, axis, steps):
    count = lax.axis_size(axis)
    first, last = (max(0, -steps), min(count, count - steps))
    return lax.ppermute(value, axis, [(source, source + steps) for source in range(first, last)])


def swapped(value, axis, bits):
    return lax.ppermute(value, axis, [(i, i ^ bits) for i in range(lax.axis_size(axis))])


def ring_move(value, axis, cross):
    chips = lax.axis_size(axis) // 2
    pairs = []
    for chip in range(chips):
        for core in range(2):
            source_chip = (chip + (-1 if core == 0 else 1)) % chips
            pairs.append((2 * source_chip + (core ^ cross), 2 * chip + core))
    return lax.ppermute(value, axis, pairs)


def group_lanes(channels, first):
    lane = lax.broadcasted_iota(jnp.int32, (channels, 128), 1)
    group = lax.broadcasted_iota(jnp.int32, (channels, 128), 0) // (channels // GROUPS) + first
    return (lane == group).astype(F32)


def exact_dot(lhs, rhs):
    return lax.dot_general(
        lhs,
        rhs,
        (((1,), (0,)), ((), ())),
        precision=lax.Precision.HIGHEST,
        preferred_element_type=F32,
    )


def pack_kernel(ids, valid, feat, gain, bias, table, params, kept):
    frames, height, across, channels = feat.shape
    kept[...] = feat[...]
    params[0:1, :] = gain[...]
    params[1:2, :] = bias[...]

    first, second = [], []
    for f in range(frames):
        block = feat[f].astype(F32).reshape(height * across, channels)
        first.append(jnp.sum(block, axis=0, keepdims=True))
        second.append(jnp.sum(block * block, axis=0, keepdims=True))
    rows = exact_dot(
        jnp.concatenate(first + first, axis=0), group_lanes(channels, 0)
    ) + exact_dot(jnp.concatenate(second + second, axis=0), group_lanes(channels, GROUPS))
    lane = lax.broadcasted_iota(jnp.int32, (1, 128), 1)
    for at in range(2 * frames):
        weight = valid[at % frames].astype(F32)
        row = rows[at : at + 1, :] * weight
        row = jnp.where(lane == ID_LANE, ids[at % frames].astype(F32) + 1.0, row)
        table[at : at + 1, :] = jnp.where(lane == VALID_LANE, weight, row)


def pack_call(clip_ids, frame_valid, features, gain, bias):
    frames, channels = features.shape[0], features.shape[-1]
    vmem = pl.BlockSpec(memory_space=pltpu.VMEM)
    return pl.pallas_call(
        pack_kernel,
        out_shape=(
            jax.ShapeDtypeStruct((2 * frames, 128), F32),
            jax.ShapeDtypeStruct((8, channels), F32),
            jax.ShapeDtypeStruct(features.shape, BF16),
        ),
        in_specs=[pl.BlockSpec(memory_space=pltpu.SMEM)] * 2 + [vmem] * 3,
        out_specs=(vmem,) * 3,
        compiler_params=pltpu.CompilerParams(vmem_limit_bytes=24 << 20),
        name="frame_sums",
    )(clip_ids, frame_valid, features, gain, bias)


def edges_kernel(place, feat, prev, plain, swap, edge):
    frames, height, across, channels = feat.shape
    taps, slice_in, _ = plain.shape
    swap[0:taps] = plain[...]
    for core in range(2):

        @pl.when(place[0] % 2 == core)
        def _(core=core):
            for source, first, count in ((prev, 0, 2), (feat, 2, frames)):
                first_rows = source[:, 0:2].reshape(count, slice_in, channels)
                last_rows = source[:, height - 2 :].reshape(count, slice_in, channels)
                edge[first : first + count] = last_rows if core else first_rows
                swap[taps + first : taps + first + count] = first_rows if core else last_rows


def edges_call(place, feat, prev, plain):
    frames, height, across, channels = feat.shape
    taps, slice_in, _ = plain.shape
    vmem = pl.BlockSpec(memory_space=pltpu.VMEM)
    return pl.pallas_call(
        edges_kernel,
        out_shape=(
            jax.ShapeDtypeStruct((taps + frames + 2, slice_in, channels), BF16),
            jax.ShapeDtypeStruct((frames + 2, slice_in, channels), BF16),
        ),
        in_specs=[pl.BlockSpec(memory_space=pltpu.SMEM)] + [vmem] * 3,
        out_specs=(vmem,) * 2,
        compiler_params=pltpu.CompilerParams(vmem_limit_bytes=16 << 20),
        name="edge_rows",
    )(place, feat, prev, plain)


def held_places(band):
    chip, core = band // 2, band % 2
    near_chip = (chip + 3 + 2 * core) % 4
    far_chip = (chip + 2) % 4
    return [band, 2 * near_chip + core, 2 * near_chip + 1 - core, 2 * far_chip + core]


def main_kernel(place, block, params, feat, prev, edge, *rest):
    pieces, (out, w_all, hcol, mixed_all, top, bottom, sems) = rest[:8], rest[8:]
    frames, height, across, channels = feat.shape
    taps, slice_in = pieces[0].shape[:2]
    taps_conv = 27

    band = place[0]
    places = held_places(band) + held_places(band + 1 - 2 * (band % 2))
    copies = []
    for at in range(8):
        start = pl.multiple_of(places[at] * slice_in, slice_in)
        source, target = pieces[at].at[0:taps], w_all.at[:, pl.ds(start, slice_in), :]
        copies.append(pltpu.make_async_copy(source, target, sems.at[at]))
    for copy in copies:
        copy.start()

    swap = pieces[4]
    for core in range(2):

        @pl.when(band % 2 == core)
        def _(core=core):
            swap_rows = swap[taps:].reshape(frames + 2, 2, across, channels)
            edge_rows = edge[...].reshape(frames + 2, 2, across, channels)
            top[...] = (swap_rows if core else edge_rows)[:, 1:2]
            bottom[...] = edge_rows if core else swap_rows

    bands = block.shape[1]
    here = place[1] % BLOCK

    def lane_of(rows, at):
        lane = lax.broadcasted_iota(jnp.int32, rows.shape, 1)
        return jnp.sum(jnp.where(lane == at, rows, 0.0), axis=1, keepdims=True)

    own_rows = block[here, 0]
    own_ids = lane_of(own_rows, ID_LANE)
    own_valid = lane_of(own_rows, VALID_LANE)
    total = jnp.zeros((8, 128), F32)
    for device in range(BLOCK):
        table = block[device, 0]
        table_ids = lane_of(table, ID_LANE)
        for sender in range(1, bands):
            table = table + block[device, sender]
        for f in range(2 * frames):
            same = table_ids[f : f + 1] == own_ids
            total = total + jnp.where(same, table[f : f + 1, :], 0.0)
    group = channels // GROUPS
    count = lane_of(total, VALID_LANE) * float(height * across * group)
    safe = jnp.maximum(count, 1.0)
    both = total / safe
    lane_at = lax.broadcasted_iota(jnp.int32, (128, channels), 0)
    group_at = lax.broadcasted_iota(jnp.int32, (128, channels), 1) // group
    mean = exact_dot(both, (lane_at == group_at).astype(F32))
    square = exact_dot(both, (lane_at == group_at + GROUPS).astype(F32))
    variance = jnp.maximum(square - mean * mean, 0.0)
    half_scale = 0.5 * (lax.rsqrt(variance + 1e-05) * params[0:1, :])
    half_bias = 0.5 * params[1:2, :]

    before_own = block[jnp.maximum(here - 1, 0), 0][frames - 2 : frames]
    before_sent = block[BLOCK - 1, 0][2 * frames - 2 : 2 * frames]
    before_rows = jnp.where(here > 0, before_own, before_sent)
    before_ids = lane_of(before_rows, ID_LANE)
    before_valid = lane_of(before_rows, VALID_LANE)

    top_ok = (band > 0).astype(F32)
    bottom_ok = (band < bands - 1).astype(F32)

    def normalise(x, at, weight, j, first, inside=None):
        rows = x.shape[0]
        x = x.astype(F32).reshape(rows * across, channels)
        u = (x - mean[at : at + 1]) * half_scale[at : at + 1] + half_bias
        h = (u + u * jnp.tanh(u)) * weight
        if inside is not None:
            h = jnp.where(jnp.full(h.shape, inside) > 0.0, h, 0.0)
        column = lax.broadcasted_iota(jnp.int32, h.shape, 0) % across
        left = jnp.where(column == 0, 0.0, pltpu.roll(h, 1, 0))
        right = jnp.where(column == across - 1, 0.0, pltpu.roll(h, rows * across - 1, 0))
        shape = (rows, across, channels)
        hcol[j, pl.ds(first, rows), :, 0:channels] = left.astype(BF16).reshape(shape)
        hcol[j, pl.ds(first, rows), :, channels : 2 * channels] = h.astype(BF16).reshape(shape)
        hcol[j, pl.ds(first, rows), :, 2 * channels :] = right.astype(BF16).reshape(shape)

    rows_step = 4
    for j in range(frames + 2):
        at = max(j - 2, 0)
        if j < 2:
            weight = before_valid[j : j + 1]
            source, source_at = prev, j
        else:
            weight = own_valid[at : at + 1]
            source, source_at = feat, at
        normalise(top[j], at, weight, j, 0, top_ok)
        normalise(bottom[j], at, weight, j, height + 1, bottom_ok)

        @pl.loop(0, height // rows_step)
        def _(step):
            first = step * rows_step
            x = source[source_at, pl.ds(first, rows_step)]
            normalise(x, at, weight, j, first + 1)

    for copy in copies:
        copy.wait()

    out_rows = height + 1
    lane_parts = channels // 128
    ids_all = [before_ids[f : f + 1] for f in range(2)]
    ids_all = ids_all + [own_ids[f : f + 1] for f in range(frames)]
    for t in range(frames):
        total = None
        for dt in (2, 1, 0):
            part = None
            for dr in range(3):
                lhs = hcol[t + dt, dr : dr + out_rows].reshape(out_rows * across, 3 * channels)
                tap = (dt * 3 + dr) * 3
                rhs = w_all[tap : tap + 3].reshape(3 * channels, channels)
                product = jnp.dot(lhs, rhs, preferred_element_type=F32)
                part = product if part is None else part + product
            if dt == 2:
                total = part
            else:
                total = total + jnp.where(ids_all[t + dt] == ids_all[t + 2], part, 0.0)
        weight = own_valid[t : t + 1]
        body_rows = height * across
        main_rows = feat[t].astype(F32).reshape(body_rows, channels) + total[:body_rows]
        main_rows = (weight * main_rows).astype(BF16).astype(F32)
        main_rows = main_rows.reshape(height // 2, 2, across, channels)
        last_row = bottom[2 + t, 0].astype(F32) + total[body_rows:]
        last_row = (weight * last_row * bottom_ok).astype(BF16).astype(F32)
        for part_at in range(lane_parts):
            lanes = slice(part_at * 128, (part_at + 1) * 128)
            mixed_all[part_at, t, 0 : height // 2] = main_rows[..., lanes]
            mixed_all[part_at, t, height // 2, 0] = last_row[:, lanes]

    half_rows, half_across = height // 2, across // 2
    points = frames * half_rows * half_across
    reduced = None
    for dr in range(3):
        rows_at, parity = (1 if dr == 2 else 0), dr % 2

        def every_second(first):
            columns = pl.ds(first, half_across, 2)
            return jnp.concatenate(
                [
                    mixed_all[at, :, rows_at : rows_at + half_rows, parity, columns, :].reshape(
                        points, 128
                    )
                    for at in range(lane_parts)
                ],
                axis=-1,
            )

        even, odd = every_second(0), every_second(1)
        column = lax.broadcasted_iota(jnp.int32, even.shape, 0) % half_across
        following = jnp.where(column == half_across - 1, 0.0, pltpu.roll(even, points - 1, 0))
        lhs = jnp.concatenate([even, odd, following], axis=-1).astype(BF16)
        tap = taps_conv + dr * 3
        rhs = w_all[tap : tap + 3].reshape(3 * channels, channels)
        product = jnp.dot(lhs, rhs, preferred_element_type=F32)
        reduced = product if reduced is None else reduced + product
    out[...] = reduced.astype(BF16)


def main_call(place, block, params, feat, prev, edge, pieces):
    frames, height, across, channels = feat.shape
    taps = pieces[0].shape[0]
    points = frames * (height // 2) * (across // 2)
    vmem = pl.BlockSpec(memory_space=pltpu.VMEM)
    return pl.pallas_call(
        main_kernel,
        out_shape=jax.ShapeDtypeStruct((points, channels), BF16),
        in_specs=[pl.BlockSpec(memory_space=pltpu.SMEM)]
        + [vmem] * 13,
        out_specs=vmem,
        scratch_shapes=[
            pltpu.VMEM((taps, channels, channels), BF16),
            pltpu.VMEM((frames + 2, height + 3, across, 3 * channels), BF16),
            pltpu.VMEM((channels // 128, frames, height // 2 + 1, 2, across, 128), F32),
            pltpu.VMEM((frames + 2, 1, across, channels), BF16),
            pltpu.VMEM((frames + 2, 2, across, channels), BF16),
            pltpu.SemaphoreType.DMA((8,)),
        ],
        compiler_params=pltpu.CompilerParams(vmem_limit_bytes=28 << 20),
        name="norm_conv_down",
    )(place, block, params, feat, prev, edge, *pieces)


def body(features, clip_ids, frame_valid, norm_gain, norm_bias, conv_weight, down_weight):
    frames, height, across, channels = features.shape
    slice_in = conv_weight.shape[3]
    place = jnp.stack([lax.axis_index("rows"), lax.axis_index("tm")]).astype(jnp.int32)

    bands, times = lax.axis_size("rows"), lax.axis_size("tm")

    prev = shifted(features[frames - 2 :], "tm", 1)
    plain = jnp.concatenate(
        [
            conv_weight.reshape(27, slice_in, channels),
            down_weight.reshape(9, slice_in, channels),
        ],
        axis=0,
    )
    near = ring_move(plain, "rows", 0)
    table, params, feat = pack_call(
        clip_ids,
        frame_valid,
        features,
        norm_gain.reshape(1, channels),
        norm_bias.reshape(1, channels),
    )
    near_cross = ring_move(plain, "rows", 1)

    half = BLOCK // 2
    pairs = [(at, at + (BLOCK if at % BLOCK >= half else -BLOCK)) for at in range(times)]
    sent = lax.ppermute(table, "tm", [pair for pair in pairs if 0 <= pair[1] < times])
    row = lax.broadcasted_iota(jnp.int32, table.shape, 0)
    rows = jnp.where(row < frames, table, sent)

    near, prev, rows = lax.optimization_barrier((near, prev, rows))
    far = ring_move(near, "rows", 0)
    near_swapped = swapped(near, "rows", 1)
    swap, edge = edges_call(place, feat, prev, plain)
    other = swapped(swap, "rows", 1)
    edge = ring_move(edge, "rows", 1)
    near_cross, rows = lax.optimization_barrier((near_cross, rows))
    cross_swapped = swapped(near_cross, "rows", 1)

    size = BLOCK * bands
    groups = [[first + at for at in range(size)] for first in range(0, bands * times, size)]
    block = lax.all_to_all(
        jnp.broadcast_to(rows[None], (size, *rows.shape)),
        ("tm", "rows"),
        0,
        0,
        axis_index_groups=groups,
        tiled=True,
    ).reshape(BLOCK, bands, *rows.shape)

    far, block = lax.optimization_barrier((far, block))
    far_swapped = swapped(far, "rows", 1)
    pieces = [plain, near, near_cross, far, other, near_swapped, cross_swapped, far_swapped]

    out = main_call(place, block, params, feat, prev, edge, pieces)
    return out.reshape(frames, height // 2, across // 2, channels)


def solution(mesh):
    return jax.shard_map(
        body,
        mesh=mesh,
        in_specs=(
            P("tm", "rows", None, None),
            P("tm"),
            P("tm"),
            P(),
            P(),
            P(None, None, None, "rows", None),
            P(None, None, "rows", None),
        ),
        out_specs=P("tm", "rows", None, None),
        check_vma=False,
    )
```

```python
import jax
import jax.numpy as jnp
from jax import lax
from jax.experimental import pallas as pl
from jax.experimental.pallas import tpu as pltpu
from jax.sharding import PartitionSpec as P

GROUPS = 32
ID_LANE = 64
VALID_LANE = 65
BLOCK = 4
F32 = jnp.float32
BF16 = jnp.bfloat16


def shifted(value, axis, steps):
    count = lax.axis_size(axis)
    first, last = (max(0, -steps), min(count, count - steps))
    return lax.ppermute(value, axis, [(source, source + steps) for source in range(first, last)])


def swapped(value, axis, bits):
    return lax.ppermute(value, axis, [(i, i ^ bits) for i in range(lax.axis_size(axis))])


def ring_move(value, axis, cross):
    chips = lax.axis_size(axis) // 2
    pairs = []
    for chip in range(chips):
        for core in range(2):
            source_chip = (chip + (-1 if core == 0 else 1)) % chips
            pairs.append((2 * source_chip + (core ^ cross), 2 * chip + core))
    return lax.ppermute(value, axis, pairs)


def group_lanes(channels, first):
    lane = lax.broadcasted_iota(jnp.int32, (channels, 128), 1)
    group = lax.broadcasted_iota(jnp.int32, (channels, 128), 0) // (channels // GROUPS) + first
    return (lane == group).astype(F32)


def exact_dot(lhs, rhs):
    return lax.dot_general(
        lhs,
        rhs,
        (((1,), (0,)), ((), ())),
        precision=lax.Precision.HIGHEST,
        preferred_element_type=F32,
    )


def pack_kernel(ids, valid, feat, gain, bias, table, params, kept):
    frames, height, across, channels = feat.shape
    kept[...] = feat[...]
    params[0:1, :] = gain[...]
    params[1:2, :] = bias[...]

    first, second = [], []
    for f in range(frames):
        block = feat[f].astype(F32).reshape(height * across, channels)
        first.append(jnp.sum(block, axis=0, keepdims=True))
        second.append(jnp.sum(block * block, axis=0, keepdims=True))
    rows = exact_dot(
        jnp.concatenate(first + first, axis=0), group_lanes(channels, 0)
    ) + exact_dot(jnp.concatenate(second + second, axis=0), group_lanes(channels, GROUPS))
    lane = lax.broadcasted_iota(jnp.int32, (1, 128), 1)
    for at in range(2 * frames):
        weight = valid[at % frames].astype(F32)
        row = rows[at : at + 1, :] * weight
        row = jnp.where(lane == ID_LANE, ids[at % frames].astype(F32) + 1.0, row)
        table[at : at + 1, :] = jnp.where(lane == VALID_LANE, weight, row)


def pack_call(clip_ids, frame_valid, features, gain, bias):
    frames, channels = features.shape[0], features.shape[-1]
    vmem = pl.BlockSpec(memory_space=pltpu.VMEM)
    return pl.pallas_call(
        pack_kernel,
        out_shape=(
            jax.ShapeDtypeStruct((2 * frames, 128), F32),
            jax.ShapeDtypeStruct((8, channels), F32),
            jax.ShapeDtypeStruct(features.shape, BF16),
        ),
        in_specs=[pl.BlockSpec(memory_space=pltpu.SMEM)] * 2 + [vmem] * 3,
        out_specs=(vmem,) * 3,
        compiler_params=pltpu.CompilerParams(vmem_limit_bytes=10 << 20),
        name="frame_sums",
    )(clip_ids, frame_valid, features, gain, bias)


def swap_kernel(place, feat, prev, plain, near, near_cross, swap, edge):
    frames, height, across, channels = feat.shape
    taps, slice_in, _ = plain.shape
    for at, piece in enumerate((plain, near, near_cross)):
        swap[at * taps : (at + 1) * taps] = piece[...]
    for core in range(2):

        @pl.when(place[0] % 2 == core)
        def _(core=core):
            for source, first, count in ((prev, 0, 2), (feat, 2, frames)):
                first_rows = source[:, 0:2].reshape(count, slice_in, channels)
                last_rows = source[:, height - 2 :].reshape(count, slice_in, channels)
                edge[first : first + count] = last_rows if core else first_rows
                to_core = first_rows if core else last_rows
                swap[3 * taps + first : 3 * taps + first + count] = to_core


def swap_call(place, feat, prev, plain, near, near_cross):
    frames, height, across, channels = feat.shape
    taps, slice_in, _ = plain.shape
    vmem = pl.BlockSpec(memory_space=pltpu.VMEM)
    return pl.pallas_call(
        swap_kernel,
        out_shape=(
            jax.ShapeDtypeStruct((3 * taps + frames + 2, slice_in, channels), BF16),
            jax.ShapeDtypeStruct((frames + 2, slice_in, channels), BF16),
        ),
        in_specs=[pl.BlockSpec(memory_space=pltpu.SMEM)] + [vmem] * 5,
        out_specs=(vmem,) * 2,
        compiler_params=pltpu.CompilerParams(vmem_limit_bytes=10 << 20),
        name="swap_message",
    )(place, feat, prev, plain, near, near_cross)


def held_places(band):
    chip, core = band // 2, band % 2
    near_chip = (chip + 3 + 2 * core) % 4
    far_chip = (chip + 2) % 4
    return [band, 2 * near_chip + core, 2 * near_chip + 1 - core, 2 * far_chip + core]


def main_kernel(place, block, params, feat, prev, edge, *rest):
    swap, pieces = rest[0], rest[1:6]
    out, w_all, hcol, mixed_all, top, bottom, sems = rest[6:]
    frames, height, across, channels = feat.shape
    taps, slice_in = pieces[0].shape[:2]
    taps_conv = 27

    band = place[0]
    places = held_places(band) + held_places(band + 1 - 2 * (band % 2))
    sources = list(pieces[:4])
    sources += [swap.at[at * taps : (at + 1) * taps] for at in range(3)] + [pieces[4]]
    copies = []
    for at in range(8):
        start = pl.multiple_of(places[at] * slice_in, slice_in)
        source, target = sources[at], w_all.at[:, pl.ds(start, slice_in), :]
        copies.append(pltpu.make_async_copy(source, target, sems.at[at]))
    for copy in copies:
        copy.start()

    for core in range(2):

        @pl.when(band % 2 == core)
        def _(core=core):
            swap_rows = swap[3 * taps :].reshape(frames + 2, 2, across, channels)
            edge_rows = edge[...].reshape(frames + 2, 2, across, channels)
            top[...] = (swap_rows if core else edge_rows)[:, 1:2]
            bottom[...] = edge_rows if core else swap_rows

    bands = block.shape[1]
    here = place[1] % BLOCK

    def lane_of(rows, at):
        lane = lax.broadcasted_iota(jnp.int32, rows.shape, 1)
        return jnp.sum(jnp.where(lane == at, rows, 0.0), axis=1, keepdims=True)

    own_rows = block[here, 0]
    own_ids = lane_of(own_rows, ID_LANE)
    own_valid = lane_of(own_rows, VALID_LANE)
    total = jnp.zeros((8, 128), F32)
    for device in range(BLOCK):
        table = block[device, 0]
        table_ids = lane_of(table, ID_LANE)
        for sender in range(1, bands):
            table = table + block[device, sender]
        for f in range(2 * frames):
            same = table_ids[f : f + 1] == own_ids
            total = total + jnp.where(same, table[f : f + 1, :], 0.0)
    group = channels // GROUPS
    count = lane_of(total, VALID_LANE) * float(height * across * group)
    safe = jnp.maximum(count, 1.0)
    both = total / safe
    lane_at = lax.broadcasted_iota(jnp.int32, (128, channels), 0)
    group_at = lax.broadcasted_iota(jnp.int32, (128, channels), 1) // group
    mean = exact_dot(both, (lane_at == group_at).astype(F32))
    square = exact_dot(both, (lane_at == group_at + GROUPS).astype(F32))
    variance = jnp.maximum(square - mean * mean, 0.0)
    half_scale = 0.5 * (lax.rsqrt(variance + 1e-05) * params[0:1, :])
    half_bias = 0.5 * params[1:2, :]

    before_own = block[jnp.maximum(here - 1, 0), 0][frames - 2 : frames]
    before_sent = block[BLOCK - 1, 0][2 * frames - 2 : 2 * frames]
    before_rows = jnp.where(here > 0, before_own, before_sent)
    before_ids = lane_of(before_rows, ID_LANE)
    before_valid = lane_of(before_rows, VALID_LANE)

    top_ok = (band > 0).astype(F32)
    bottom_ok = (band < bands - 1).astype(F32)

    def normalise(x, at, weight, j, first, inside=None):
        rows = x.shape[0]
        x = x.astype(F32).reshape(rows * across, channels)
        u = (x - mean[at : at + 1]) * half_scale[at : at + 1] + half_bias
        h = (u + u * jnp.tanh(u)) * weight
        if inside is not None:
            h = jnp.where(jnp.full(h.shape, inside) > 0.0, h, 0.0)
        column = lax.broadcasted_iota(jnp.int32, h.shape, 0) % across
        left = jnp.where(column == 0, 0.0, pltpu.roll(h, 1, 0))
        right = jnp.where(column == across - 1, 0.0, pltpu.roll(h, rows * across - 1, 0))
        shape = (rows, across, channels)
        hcol[j, pl.ds(first, rows), :, 0:channels] = left.astype(BF16).reshape(shape)
        hcol[j, pl.ds(first, rows), :, channels : 2 * channels] = h.astype(BF16).reshape(shape)
        hcol[j, pl.ds(first, rows), :, 2 * channels :] = right.astype(BF16).reshape(shape)

    rows_step = 4
    for j in range(frames + 2):
        at = max(j - 2, 0)
        if j < 2:
            weight = before_valid[j : j + 1]
            source, source_at = prev, j
        else:
            weight = own_valid[at : at + 1]
            source, source_at = feat, at
        normalise(top[j], at, weight, j, 0, top_ok)
        normalise(bottom[j], at, weight, j, height + 1, bottom_ok)

        @pl.loop(0, height // rows_step)
        def _(step):
            first = step * rows_step
            x = source[source_at, pl.ds(first, rows_step)]
            normalise(x, at, weight, j, first + 1)

    for copy in copies:
        copy.wait()

    out_rows = height + 1
    lane_parts = channels // 128
    ids_all = [before_ids[f : f + 1] for f in range(2)]
    ids_all = ids_all + [own_ids[f : f + 1] for f in range(frames)]
    for t in range(frames):
        total = None
        for dt in (2, 1, 0):
            lhs = jnp.concatenate(
                [
                    hcol[t + dt, dr : dr + out_rows].reshape(out_rows * across, 3 * channels)
                    for dr in range(3)
                ],
                axis=1,
            )
            rhs = w_all[dt * 9 : dt * 9 + 9].reshape(9 * channels, channels)
            part = jnp.dot(lhs, rhs, preferred_element_type=F32)
            if dt == 2:
                total = part
            else:
                total = total + jnp.where(ids_all[t + dt] == ids_all[t + 2], part, 0.0)
        weight = own_valid[t : t + 1]
        body_rows = height * across
        main_rows = feat[t].astype(F32).reshape(body_rows, channels) + total[:body_rows]
        main_rows = (weight * main_rows).astype(BF16).astype(F32)
        main_rows = main_rows.reshape(height // 2, 2, across, channels)
        last_row = bottom[2 + t, 0].astype(F32) + total[body_rows:]
        last_row = (weight * last_row * bottom_ok).astype(BF16).astype(F32)
        for part_at in range(lane_parts):
            lanes = slice(part_at * 128, (part_at + 1) * 128)
            mixed_all[part_at, t, 0 : height // 2] = main_rows[..., lanes]
            mixed_all[part_at, t, height // 2, 0] = last_row[:, lanes]

    half_rows, half_across = height // 2, across // 2
    points = frames * half_rows * half_across
    reduced = None
    for dr in range(3):
        rows_at, parity = (1 if dr == 2 else 0), dr % 2

        def every_second(first):
            columns = pl.ds(first, half_across, 2)
            return jnp.concatenate(
                [
                    mixed_all[at, :, rows_at : rows_at + half_rows, parity, columns, :].reshape(
                        points, 128
                    )
                    for at in range(lane_parts)
                ],
                axis=-1,
            )

        even, odd = every_second(0), every_second(1)
        column = lax.broadcasted_iota(jnp.int32, even.shape, 0) % half_across
        following = jnp.where(column == half_across - 1, 0.0, pltpu.roll(even, points - 1, 0))
        lhs = jnp.concatenate([even, odd, following], axis=-1).astype(BF16)
        tap = taps_conv + dr * 3
        rhs = w_all[tap : tap + 3].reshape(3 * channels, channels)
        product = jnp.dot(lhs, rhs, preferred_element_type=F32)
        reduced = product if reduced is None else reduced + product
    out[...] = reduced.astype(BF16)


def main_call(place, block, params, feat, prev, edge, swap, pieces):
    frames, height, across, channels = feat.shape
    taps = pieces[0].shape[0]
    points = frames * (height // 2) * (across // 2)
    vmem = pl.BlockSpec(memory_space=pltpu.VMEM)
    return pl.pallas_call(
        main_kernel,
        out_shape=jax.ShapeDtypeStruct((points, channels), BF16),
        in_specs=[pl.BlockSpec(memory_space=pltpu.SMEM)]
        + [vmem] * 11,
        out_specs=vmem,
        scratch_shapes=[
            pltpu.VMEM((taps, channels, channels), BF16),
            pltpu.VMEM((frames + 2, height + 3, across, 3 * channels), BF16),
            pltpu.VMEM((channels // 128, frames, height // 2 + 1, 2, across, 128), F32),
            pltpu.VMEM((frames + 2, 1, across, channels), BF16),
            pltpu.VMEM((frames + 2, 2, across, channels), BF16),
            pltpu.SemaphoreType.DMA((8,)),
        ],
        compiler_params=pltpu.CompilerParams(vmem_limit_bytes=24 << 20),
        name="norm_conv_down",
    )(place, block, params, feat, prev, edge, swap, *pieces)


def body(features, clip_ids, frame_valid, norm_gain, norm_bias, conv_weight, down_weight):
    frames, height, across, channels = features.shape
    slice_in = conv_weight.shape[3]
    place = jnp.stack([lax.axis_index("rows"), lax.axis_index("tm")]).astype(jnp.int32)

    bands, times = lax.axis_size("rows"), lax.axis_size("tm")

    prev = shifted(features[frames - 2 :], "tm", 1)
    plain = jnp.concatenate(
        [
            conv_weight.reshape(27, slice_in, channels),
            down_weight.reshape(9, slice_in, channels),
        ],
        axis=0,
    )
    near = ring_move(plain, "rows", 0)
    table, params, feat = pack_call(
        clip_ids,
        frame_valid,
        features,
        norm_gain.reshape(1, channels),
        norm_bias.reshape(1, channels),
    )
    near_cross = ring_move(plain, "rows", 1)

    half = BLOCK // 2
    pairs = [(at, at + (BLOCK if at % BLOCK >= half else -BLOCK)) for at in range(times)]
    sent = lax.ppermute(table, "tm", [pair for pair in pairs if 0 <= pair[1] < times])
    row = lax.broadcasted_iota(jnp.int32, table.shape, 0)
    rows = jnp.where(row < frames, table, sent)

    near, prev, rows = lax.optimization_barrier((near, prev, rows))
    far = ring_move(near, "rows", 0)
    swap, edge = swap_call(place, feat, prev, plain, near, near_cross)
    swap = swapped(swap, "rows", 1)
    edge = ring_move(edge, "rows", 1)

    size = BLOCK * bands
    groups = [[first + at for at in range(size)] for first in range(0, bands * times, size)]
    block = lax.all_to_all(
        jnp.broadcast_to(rows[None], (size, *rows.shape)),
        ("tm", "rows"),
        0,
        0,
        axis_index_groups=groups,
        tiled=True,
    ).reshape(BLOCK, bands, *rows.shape)

    far, block, edge = lax.optimization_barrier((far, block, edge))
    pieces = [plain, near, near_cross, far, swapped(far, "rows", 1)]

    out = main_call(place, block, params, feat, prev, edge, swap, pieces)
    return out.reshape(frames, height // 2, across // 2, channels)


def solution(mesh):
    return jax.shard_map(
        body,
        mesh=mesh,
        in_specs=(
            P("tm", "rows", None, None),
            P("tm"),
            P("tm"),
            P(),
            P(),
            P(None, None, None, "rows", None),
            P(None, None, "rows", None),
        ),
        out_specs=P("tm", "rows", None, None),
        check_vma=False,
    )
```

```python
import jax
import jax.numpy as jnp
from jax import lax
from jax.experimental import pallas as pl
from jax.experimental.pallas import tpu as pltpu
from jax.sharding import PartitionSpec as P

GROUPS = 32
ID_LANE = 64
VALID_LANE = 65
BLOCK = 4
F32 = jnp.float32
BF16 = jnp.bfloat16


def shifted(value, axis, steps):
    count = lax.axis_size(axis)
    first, last = (max(0, -steps), min(count, count - steps))
    return lax.ppermute(value, axis, [(source, source + steps) for source in range(first, last)])


def swapped(value, axis, bits):
    return lax.ppermute(value, axis, [(i, i ^ bits) for i in range(lax.axis_size(axis))])


def ring_pairs(bands, cross):
    chips = bands // 2
    pairs = []
    for chip in range(chips):
        for core in range(2):
            source_chip = (chip + (-1 if core == 0 else 1)) % chips
            pairs.append((2 * source_chip + (core ^ cross), 2 * chip + core))
    return pairs


def ring_move(value, cross):
    return lax.ppermute(value, "rows", ring_pairs(lax.axis_size("rows"), cross))


def diagonal_move(value, band_pairs):
    bands, times = lax.axis_size("rows"), lax.axis_size("tm")
    pairs = [
        ((at - 1) * bands + source, at * bands + target)
        for at in range(1, times)
        for source, target in band_pairs
    ]
    return lax.ppermute(value, ("tm", "rows"), pairs)


def group_lanes(channels, first):
    lane = lax.broadcasted_iota(jnp.int32, (channels, 128), 1)
    group = lax.broadcasted_iota(jnp.int32, (channels, 128), 0) // (channels // GROUPS) + first
    return (lane == group).astype(F32)


def exact_dot(lhs, rhs):
    return lax.dot_general(
        lhs,
        rhs,
        (((1,), (0,)), ((), ())),
        precision=lax.Precision.HIGHEST,
        preferred_element_type=F32,
    )


def pack_kernel(
    place, feat, norm, table, params, kept, tail, chip_edge, core_edge, chip_last, core_last
):
    frames, height, across, channels = feat.shape
    kept[...] = feat[...]
    tail[...] = feat[frames - 2 :]
    for core in range(2):

        @pl.when(place[0] % 2 == core)
        def _(core=core):
            sides = ((chip_edge, chip_last, core), (core_edge, core_last, 1 - core))
            for target, last, side in sides:
                row = side * (height - 2)
                target[...] = feat[:, row : row + 2].reshape(target.shape)
                last[...] = feat[frames - 2 :, row : row + 2].reshape(last.shape)

    params[0:2, :] = norm[...]

    first, second = [], []
    for f in range(frames):
        block = feat[f].astype(F32).reshape(height * across, channels)
        first.append(jnp.sum(block, axis=0, keepdims=True))
        second.append(jnp.sum(block * block, axis=0, keepdims=True))
    rows = exact_dot(
        jnp.concatenate(first + first, axis=0), group_lanes(channels, 0)
    ) + exact_dot(jnp.concatenate(second + second, axis=0), group_lanes(channels, GROUPS))
    lane = lax.broadcasted_iota(jnp.int32, (1, 128), 1)
    for at in range(2 * frames):
        weight = place[2 + frames + at % frames].astype(F32)
        row = rows[at : at + 1, :] * weight
        row = jnp.where(lane == ID_LANE, place[2 + at % frames].astype(F32) + 1.0, row)
        table[at : at + 1, :] = jnp.where(lane == VALID_LANE, weight, row)


def pack_call(place, features, norm):
    frames, height, across, channels = features.shape
    vmem = pl.BlockSpec(memory_space=pltpu.VMEM)
    return pl.pallas_call(
        pack_kernel,
        out_shape=(
            jax.ShapeDtypeStruct((2 * frames, 128), F32),
            jax.ShapeDtypeStruct((8, channels), F32),
            jax.ShapeDtypeStruct(features.shape, BF16),
            jax.ShapeDtypeStruct((2, height, across, channels), BF16),
            jax.ShapeDtypeStruct((frames, 2 * across, channels), BF16),
            jax.ShapeDtypeStruct((frames, 2 * across, channels), BF16),
            jax.ShapeDtypeStruct((2, 2 * across, channels), BF16),
            jax.ShapeDtypeStruct((2, 2 * across, channels), BF16),
        ),
        in_specs=[pl.BlockSpec(memory_space=pltpu.SMEM)] + [vmem] * 2,
        out_specs=(vmem,) * 8,
        compiler_params=pltpu.CompilerParams(vmem_limit_bytes=12 << 20),
        name="frame_sums",
    )(place, features, norm)


def swap_kernel(core_edge, plain, near, near_cross, swap):
    taps = plain.shape[0]
    for at, piece in enumerate((plain, near, near_cross)):
        swap[at * taps : (at + 1) * taps] = piece[...]
    swap[3 * taps :] = core_edge[...]


def swap_call(core_edge, plain, near, near_cross):
    frames = core_edge.shape[0]
    taps, slice_in, channels = plain.shape
    vmem = pl.BlockSpec(memory_space=pltpu.VMEM)
    return pl.pallas_call(
        swap_kernel,
        out_shape=jax.ShapeDtypeStruct((3 * taps + frames, slice_in, channels), BF16),
        in_specs=[vmem] * 4,
        out_specs=vmem,
        compiler_params=pltpu.CompilerParams(vmem_limit_bytes=10 << 20),
        name="swap_message",
    )(core_edge, plain, near, near_cross)


def held_places(band):
    chip, core = band // 2, band % 2
    near_chip = (chip + 3 + 2 * core) % 4
    far_chip = (chip + 2) % 4
    return [band, 2 * near_chip + core, 2 * near_chip + 1 - core, 2 * far_chip + core]


def main_kernel(place, block, params, feat, prev, edges, far_chip, far_core, *rest):
    swap, pieces = rest[0], rest[1:6]
    out, w_all, hcol, mixed_all, top, bottom, sems = rest[6:]
    frames, height, across, channels = feat.shape
    taps, slice_in = pieces[0].shape[:2]
    taps_conv = 27

    band = place[0]
    places = held_places(band) + held_places(band + 1 - 2 * (band % 2))
    sources = [piece.at[0:taps] for piece in pieces[:4]]
    sources += [swap.at[at * taps : (at + 1) * taps] for at in range(3)] + [pieces[4]]
    copies = []
    for at in range(8):
        start = pl.multiple_of(places[at] * slice_in, slice_in)
        source, target = sources[at], w_all.at[:, pl.ds(start, slice_in), :]
        copies.append(pltpu.make_async_copy(source, target, sems.at[at]))
    for copy in copies:
        copy.start()

    for core in range(2):

        @pl.when(band % 2 == core)
        def _(core=core):
            swap_rows = swap[3 * taps :].reshape(frames, 2, across, channels)
            chip_rows = edges[...].reshape(frames, 2, across, channels)
            swap_prev = far_core[...].reshape(2, 2, across, channels)
            chip_prev = far_chip[...].reshape(2, 2, across, channels)
            above, below = (swap_rows, chip_rows) if core else (chip_rows, swap_rows)
            above_prev, below_prev = (swap_prev, chip_prev) if core else (chip_prev, swap_prev)
            top[0:2] = above_prev[:, 1:2]
            top[2:] = above[:, 1:2]
            bottom[0:2] = below_prev
            bottom[2:] = below

    bands = block.shape[1]
    here = place[1] % BLOCK

    def lane_of(rows, at):
        lane = lax.broadcasted_iota(jnp.int32, rows.shape, 1)
        return jnp.sum(jnp.where(lane == at, rows, 0.0), axis=1, keepdims=True)

    own_rows = block[here, 0]
    own_ids = lane_of(own_rows, ID_LANE)
    own_valid = lane_of(own_rows, VALID_LANE)
    total = jnp.zeros((8, 128), F32)
    for device in range(BLOCK):
        table = block[device, 0]
        table_ids = lane_of(table, ID_LANE)
        for sender in range(1, bands):
            table = table + block[device, sender]
        for f in range(2 * frames):
            same = table_ids[f : f + 1] == own_ids
            total = total + jnp.where(same, table[f : f + 1, :], 0.0)
    group = channels // GROUPS
    count = lane_of(total, VALID_LANE) * float(height * across * group)
    safe = jnp.maximum(count, 1.0)
    both = total / safe
    lane_at = lax.broadcasted_iota(jnp.int32, (128, channels), 0)
    group_at = lax.broadcasted_iota(jnp.int32, (128, channels), 1) // group
    mean = exact_dot(both, (lane_at == group_at).astype(F32))
    square = exact_dot(both, (lane_at == group_at + GROUPS).astype(F32))
    variance = jnp.maximum(square - mean * mean, 0.0)
    half_scale = 0.5 * (lax.rsqrt(variance + 1e-05) * params[0:1, :])
    half_bias = 0.5 * params[1:2, :]

    before_own = block[jnp.maximum(here - 1, 0), 0][frames - 2 : frames]
    before_sent = block[BLOCK - 1, 0][2 * frames - 2 : 2 * frames]
    before_rows = jnp.where(here > 0, before_own, before_sent)
    before_ids = lane_of(before_rows, ID_LANE)
    before_valid = lane_of(before_rows, VALID_LANE)

    top_ok = (band > 0).astype(F32)
    bottom_ok = (band < bands - 1).astype(F32)

    def normalise(x, at, weight, j, first, inside=None):
        rows = x.shape[0]
        x = x.astype(F32).reshape(rows * across, channels)
        u = (x - mean[at : at + 1]) * half_scale[at : at + 1] + half_bias
        h = (u + u * jnp.tanh(u)) * weight
        if inside is not None:
            h = jnp.where(jnp.full(h.shape, inside) > 0.0, h, 0.0)
        column = lax.broadcasted_iota(jnp.int32, h.shape, 0) % across
        left = jnp.where(column == 0, 0.0, pltpu.roll(h, 1, 0))
        right = jnp.where(column == across - 1, 0.0, pltpu.roll(h, rows * across - 1, 0))
        shape = (rows, across, channels)
        hcol[j, pl.ds(first, rows), :, 0:channels] = left.astype(BF16).reshape(shape)
        hcol[j, pl.ds(first, rows), :, channels : 2 * channels] = h.astype(BF16).reshape(shape)
        hcol[j, pl.ds(first, rows), :, 2 * channels :] = right.astype(BF16).reshape(shape)

    rows_step = 4
    for j in range(frames + 2):
        at = max(j - 2, 0)
        if j < 2:
            weight = before_valid[j : j + 1]
            source, source_at = prev, j
        else:
            weight = own_valid[at : at + 1]
            source, source_at = feat, at
        normalise(top[j], at, weight, j, 0, top_ok)
        normalise(bottom[j], at, weight, j, height + 1, bottom_ok)

        @pl.loop(0, height // rows_step)
        def _(step):
            first = step * rows_step
            x = source[source_at, pl.ds(first, rows_step)]
            normalise(x, at, weight, j, first + 1)

    for copy in copies:
        copy.wait()

    out_rows = height + 1
    lane_parts = channels // 128
    hcol[frames + 2] = jnp.zeros(hcol.shape[1:], BF16)
    ids_all = [before_ids[f, 0] for f in range(2)] + [own_ids[f, 0] for f in range(frames)]
    for t in range(frames):
        total = None
        for dt in range(3):
            at = jnp.where(ids_all[t + dt] == ids_all[t + 2], t + dt, frames + 2)
            for dr in range(3):
                lhs = hcol[at, dr : dr + out_rows].reshape(out_rows * across, 3 * channels)
                tap = (dt * 3 + dr) * 3
                rhs = w_all[tap : tap + 3].reshape(3 * channels, channels)
                product = jnp.dot(lhs, rhs, preferred_element_type=F32)
                total = product if total is None else total + product
        weight = own_valid[t : t + 1]
        body_rows = height * across
        main_rows = feat[t].astype(F32).reshape(body_rows, channels) + total[:body_rows]
        main_rows = (weight * main_rows).astype(BF16).astype(F32)
        main_rows = main_rows.reshape(height // 2, 2, across, channels)
        last_row = bottom[2 + t, 0].astype(F32) + total[body_rows:]
        last_row = (weight * last_row * bottom_ok).astype(BF16).astype(F32)
        for part_at in range(lane_parts):
            lanes = slice(part_at * 128, (part_at + 1) * 128)
            mixed_all[part_at, t, 0 : height // 2] = main_rows[..., lanes]
            mixed_all[part_at, t, height // 2, 0] = last_row[:, lanes]

    half_rows, half_across = height // 2, across // 2
    points = frames * half_rows * half_across
    reduced = None
    for dr in range(3):
        rows_at, parity = (1 if dr == 2 else 0), dr % 2

        def every_second(first):
            columns = pl.ds(first, half_across, 2)
            return jnp.concatenate(
                [
                    mixed_all[at, :, rows_at : rows_at + half_rows, parity, columns, :].reshape(
                        points, 128
                    )
                    for at in range(lane_parts)
                ],
                axis=-1,
            )

        even, odd = every_second(0), every_second(1)
        column = lax.broadcasted_iota(jnp.int32, even.shape, 0) % half_across
        following = jnp.where(column == half_across - 1, 0.0, pltpu.roll(even, points - 1, 0))
        lhs = jnp.concatenate([even, odd, following], axis=-1).astype(BF16)
        tap = taps_conv + dr * 3
        rhs = w_all[tap : tap + 3].reshape(3 * channels, channels)
        product = jnp.dot(lhs, rhs, preferred_element_type=F32)
        reduced = product if reduced is None else reduced + product
    out[...] = reduced.astype(BF16)


def main_call(place, block, params, feat, prev, edges, swap, pieces):
    frames, height, across, channels = feat.shape
    taps = pieces[0].shape[0]
    points = frames * (height // 2) * (across // 2)
    vmem = pl.BlockSpec(memory_space=pltpu.VMEM)
    return pl.pallas_call(
        main_kernel,
        out_shape=jax.ShapeDtypeStruct((points, channels), BF16),
        in_specs=[pl.BlockSpec(memory_space=pltpu.SMEM)]
        + [vmem] * 13,
        out_specs=vmem,
        scratch_shapes=[
            pltpu.VMEM((taps, channels, channels), BF16),
            pltpu.VMEM((frames + 3, height + 3, across, 3 * channels), BF16),
            pltpu.VMEM((channels // 128, frames, height // 2 + 1, 2, across, 128), F32),
            pltpu.VMEM((frames + 2, 1, across, channels), BF16),
            pltpu.VMEM((frames + 2, 2, across, channels), BF16),
            pltpu.SemaphoreType.DMA((8,)),
        ],
        compiler_params=pltpu.CompilerParams(vmem_limit_bytes=24 << 20),
        name="norm_conv_down",
    )(place, block, params, feat, prev, *edges, swap, *pieces)


def body(features, clip_ids, frame_valid, norm_gain, norm_bias, conv_weight, down_weight):
    frames, height, across, channels = features.shape
    slice_in = conv_weight.shape[3]
    where = jnp.stack([lax.axis_index("rows"), lax.axis_index("tm")]).astype(jnp.int32)
    place = jnp.concatenate([where, clip_ids, frame_valid])
    norm = jnp.stack([norm_gain, norm_bias])
    bands, times = lax.axis_size("rows"), lax.axis_size("tm")

    plain = jnp.concatenate(
        [
            conv_weight.reshape(27, slice_in, channels),
            down_weight.reshape(9, slice_in, channels),
        ],
        axis=0,
    )
    near = ring_move(plain, 0)
    table, params, feat, tail, chip_edge, core_edge, chip_last, core_last = pack_call(
        place, features, norm
    )
    prev = shifted(tail, "tm", 1)
    near_cross = ring_move(plain, 1)
    edges = [
        ring_move(chip_edge, 1),
        diagonal_move(chip_last, ring_pairs(bands, 1)),
        diagonal_move(core_last, [(at ^ 1, at) for at in range(bands)]),
    ]

    half = BLOCK // 2
    pairs = [(at, at + (BLOCK if at % BLOCK >= half else -BLOCK)) for at in range(times)]
    sent = lax.ppermute(table, "tm", [pair for pair in pairs if 0 <= pair[1] < times])
    row = lax.broadcasted_iota(jnp.int32, table.shape, 0)
    rows = jnp.where(row < frames, table, sent)

    near, prev, edges, rows = lax.optimization_barrier((near, prev, edges, rows))
    far = ring_move(near, 0)
    swap = swapped(swap_call(core_edge, plain, near, near_cross), "rows", 1)

    size = BLOCK * bands
    groups = [[first + at for at in range(size)] for first in range(0, bands * times, size)]
    block = lax.all_to_all(
        jnp.broadcast_to(rows[None], (size, *rows.shape)),
        ("tm", "rows"),
        0,
        0,
        axis_index_groups=groups,
        tiled=True,
    ).reshape(BLOCK, bands, *rows.shape)

    far, block = lax.optimization_barrier((far, block))
    pieces = [plain, near, near_cross, far, swapped(far, "rows", 1)]

    out = main_call(place, block, params, feat, prev, edges, swap, pieces)
    return out.reshape(frames, height // 2, across // 2, channels)


def solution(mesh):
    return jax.shard_map(
        body,
        mesh=mesh,
        in_specs=(
            P("tm", "rows", None, None),
            P("tm"),
            P("tm"),
            P(),
            P(),
            P(None, None, None, "rows", None),
            P(None, None, "rows", None),
        ),
        out_specs=P("tm", "rows", None, None),
        check_vma=False,
    )
```

```python
import jax
import jax.numpy as jnp
from jax import lax
from jax.experimental import pallas as pl
from jax.experimental.pallas import tpu as pltpu
from jax.sharding import PartitionSpec as P

GROUPS = 32
ID_LANE = 64
VALID_LANE = 65
BLOCK = 4
F32 = jnp.float32
BF16 = jnp.bfloat16


def shifted(value, axis, steps):
    count = lax.axis_size(axis)
    first, last = (max(0, -steps), min(count, count - steps))
    return lax.ppermute(value, axis, [(source, source + steps) for source in range(first, last)])


def swapped(value, axis, bits):
    return lax.ppermute(value, axis, [(i, i ^ bits) for i in range(lax.axis_size(axis))])


def ring_move(value, axis, cross):
    chips = lax.axis_size(axis) // 2
    pairs = []
    for chip in range(chips):
        for core in range(2):
            source_chip = (chip + (-1 if core == 0 else 1)) % chips
            pairs.append((2 * source_chip + (core ^ cross), 2 * chip + core))
    return lax.ppermute(value, axis, pairs)


def group_lanes(channels, first):
    lane = lax.broadcasted_iota(jnp.int32, (channels, 128), 1)
    group = lax.broadcasted_iota(jnp.int32, (channels, 128), 0) // (channels // GROUPS) + first
    return (lane == group).astype(F32)


def exact_dot(lhs, rhs):
    return lax.dot_general(
        lhs,
        rhs,
        (((1,), (0,)), ((), ())),
        precision=lax.Precision.HIGHEST,
        preferred_element_type=F32,
    )


def pack_kernel(ids, valid, feat, gain, bias, table, params, kept, tail):
    frames, height, across, channels = feat.shape
    kept[...] = feat[...]
    tail[...] = feat[frames - 2 :]
    params[0:1, :] = gain[...]
    params[1:2, :] = bias[...]

    first, second = [], []
    for f in range(frames):
        block = feat[f].astype(F32).reshape(height * across, channels)
        first.append(jnp.sum(block, axis=0, keepdims=True))
        second.append(jnp.sum(block * block, axis=0, keepdims=True))
    rows = exact_dot(
        jnp.concatenate(first + first, axis=0), group_lanes(channels, 0)
    ) + exact_dot(jnp.concatenate(second + second, axis=0), group_lanes(channels, GROUPS))
    lane = lax.broadcasted_iota(jnp.int32, (1, 128), 1)
    for at in range(2 * frames):
        weight = valid[at % frames].astype(F32)
        row = rows[at : at + 1, :] * weight
        row = jnp.where(lane == ID_LANE, ids[at % frames].astype(F32) + 1.0, row)
        table[at : at + 1, :] = jnp.where(lane == VALID_LANE, weight, row)


def pack_call(clip_ids, frame_valid, features, gain, bias):
    frames, channels = features.shape[0], features.shape[-1]
    vmem = pl.BlockSpec(memory_space=pltpu.VMEM)
    return pl.pallas_call(
        pack_kernel,
        out_shape=(
            jax.ShapeDtypeStruct((2 * frames, 128), F32),
            jax.ShapeDtypeStruct((8, channels), F32),
            jax.ShapeDtypeStruct(features.shape, BF16),
            jax.ShapeDtypeStruct((2, *features.shape[1:]), BF16),
        ),
        in_specs=[pl.BlockSpec(memory_space=pltpu.SMEM)] * 2 + [vmem] * 3,
        out_specs=(vmem,) * 4,
        compiler_params=pltpu.CompilerParams(vmem_limit_bytes=10 << 20),
        name="frame_sums",
    )(clip_ids, frame_valid, features, gain, bias)


def swap_kernel(place, feat, prev, plain, near, near_cross, swap, edge):
    frames, height, across, channels = feat.shape
    taps, slice_in, _ = plain.shape
    for at, piece in enumerate((plain, near, near_cross)):
        swap[at * taps : (at + 1) * taps] = piece[...]
    for core in range(2):

        @pl.when(place[0] % 2 == core)
        def _(core=core):
            for source, first, count in ((prev, 0, 2), (feat, 2, frames)):
                first_rows = source[:, 0:2].reshape(count, slice_in, channels)
                last_rows = source[:, height - 2 :].reshape(count, slice_in, channels)
                edge[first : first + count] = last_rows if core else first_rows
                to_core = first_rows if core else last_rows
                swap[3 * taps + first : 3 * taps + first + count] = to_core


def swap_call(place, feat, prev, plain, near, near_cross):
    frames, height, across, channels = feat.shape
    taps, slice_in, _ = plain.shape
    vmem = pl.BlockSpec(memory_space=pltpu.VMEM)
    return pl.pallas_call(
        swap_kernel,
        out_shape=(
            jax.ShapeDtypeStruct((3 * taps + frames + 2, slice_in, channels), BF16),
            jax.ShapeDtypeStruct((frames + 2, slice_in, channels), BF16),
        ),
        in_specs=[pl.BlockSpec(memory_space=pltpu.SMEM)] + [vmem] * 5,
        out_specs=(vmem,) * 2,
        compiler_params=pltpu.CompilerParams(vmem_limit_bytes=10 << 20),
        name="swap_message",
    )(place, feat, prev, plain, near, near_cross)


def held_places(band):
    chip, core = band // 2, band % 2
    near_chip = (chip + 3 + 2 * core) % 4
    far_chip = (chip + 2) % 4
    return [band, 2 * near_chip + core, 2 * near_chip + 1 - core, 2 * far_chip + core]


def main_kernel(place, block, params, feat, prev, edge, *rest):
    swap, pieces = rest[0], rest[1:6]
    out, w_all, hcol, mixed_all, top, bottom, sems = rest[6:]
    frames, height, across, channels = feat.shape
    taps, slice_in = pieces[0].shape[:2]
    taps_conv = 27

    band = place[0]
    places = held_places(band) + held_places(band + 1 - 2 * (band % 2))
    sources = list(pieces[:4])
    sources += [swap.at[at * taps : (at + 1) * taps] for at in range(3)] + [pieces[4]]
    copies = []
    for at in range(8):
        start = pl.multiple_of(places[at] * slice_in, slice_in)
        source, target = sources[at], w_all.at[:, pl.ds(start, slice_in), :]
        copies.append(pltpu.make_async_copy(source, target, sems.at[at]))
    for copy in copies:
        copy.start()

    for core in range(2):

        @pl.when(band % 2 == core)
        def _(core=core):
            swap_rows = swap[3 * taps :].reshape(frames + 2, 2, across, channels)
            edge_rows = edge[...].reshape(frames + 2, 2, across, channels)
            top[...] = (swap_rows if core else edge_rows)[:, 1:2]
            bottom[...] = edge_rows if core else swap_rows

    bands = block.shape[1]
    here = place[1] % BLOCK

    def lane_of(rows, at):
        lane = lax.broadcasted_iota(jnp.int32, rows.shape, 1)
        return jnp.sum(jnp.where(lane == at, rows, 0.0), axis=1, keepdims=True)

    own_rows = block[here, 0]
    own_ids = lane_of(own_rows, ID_LANE)
    own_valid = lane_of(own_rows, VALID_LANE)
    total = jnp.zeros((8, 128), F32)
    for device in range(BLOCK):
        table = block[device, 0]
        table_ids = lane_of(table, ID_LANE)
        for sender in range(1, bands):
            table = table + block[device, sender]
        for f in range(2 * frames):
            same = table_ids[f : f + 1] == own_ids
            total = total + jnp.where(same, table[f : f + 1, :], 0.0)
    group = channels // GROUPS
    count = lane_of(total, VALID_LANE) * float(height * across * group)
    safe = jnp.maximum(count, 1.0)
    both = total / safe
    lane_at = lax.broadcasted_iota(jnp.int32, (128, channels), 0)
    group_at = lax.broadcasted_iota(jnp.int32, (128, channels), 1) // group
    mean = exact_dot(both, (lane_at == group_at).astype(F32))
    square = exact_dot(both, (lane_at == group_at + GROUPS).astype(F32))
    variance = jnp.maximum(square - mean * mean, 0.0)
    half_scale = 0.5 * (lax.rsqrt(variance + 1e-05) * params[0:1, :])
    half_bias = 0.5 * params[1:2, :]

    before_own = block[jnp.maximum(here - 1, 0), 0][frames - 2 : frames]
    before_sent = block[BLOCK - 1, 0][2 * frames - 2 : 2 * frames]
    before_rows = jnp.where(here > 0, before_own, before_sent)
    before_ids = lane_of(before_rows, ID_LANE)
    before_valid = lane_of(before_rows, VALID_LANE)

    top_ok = (band > 0).astype(F32)
    bottom_ok = (band < bands - 1).astype(F32)

    def normalise(x, at, weight, j, first, inside=None):
        rows = x.shape[0]
        x = x.astype(F32).reshape(rows * across, channels)
        u = (x - mean[at : at + 1]) * half_scale[at : at + 1] + half_bias
        h = (u + u * jnp.tanh(u)) * weight
        if inside is not None:
            h = jnp.where(jnp.full(h.shape, inside) > 0.0, h, 0.0)
        column = lax.broadcasted_iota(jnp.int32, h.shape, 0) % across
        left = jnp.where(column == 0, 0.0, pltpu.roll(h, 1, 0))
        right = jnp.where(column == across - 1, 0.0, pltpu.roll(h, rows * across - 1, 0))
        shape = (rows, across, channels)
        hcol[j, pl.ds(first, rows), :, 0:channels] = left.astype(BF16).reshape(shape)
        hcol[j, pl.ds(first, rows), :, channels : 2 * channels] = h.astype(BF16).reshape(shape)
        hcol[j, pl.ds(first, rows), :, 2 * channels :] = right.astype(BF16).reshape(shape)

    rows_step = 4
    for j in range(frames + 2):
        at = max(j - 2, 0)
        if j < 2:
            weight = before_valid[j : j + 1]
            source, source_at = prev, j
        else:
            weight = own_valid[at : at + 1]
            source, source_at = feat, at
        normalise(top[j], at, weight, j, 0, top_ok)
        normalise(bottom[j], at, weight, j, height + 1, bottom_ok)

        @pl.loop(0, height // rows_step)
        def _(step):
            first = step * rows_step
            x = source[source_at, pl.ds(first, rows_step)]
            normalise(x, at, weight, j, first + 1)

    for copy in copies:
        copy.wait()

    out_rows = height + 1
    lane_parts = channels // 128
    hcol[frames + 2] = jnp.zeros(hcol.shape[1:], BF16)
    ids_all = [before_ids[f, 0] for f in range(2)] + [own_ids[f, 0] for f in range(frames)]
    for t in range(frames):
        total = None
        for dt in range(3):
            at = jnp.where(ids_all[t + dt] == ids_all[t + 2], t + dt, frames + 2)
            for dr in range(3):
                lhs = hcol[at, dr : dr + out_rows].reshape(out_rows * across, 3 * channels)
                tap = (dt * 3 + dr) * 3
                rhs = w_all[tap : tap + 3].reshape(3 * channels, channels)
                product = jnp.dot(lhs, rhs, preferred_element_type=F32)
                total = product if total is None else total + product
        weight = own_valid[t : t + 1]
        body_rows = height * across
        main_rows = feat[t].astype(F32).reshape(body_rows, channels) + total[:body_rows]
        main_rows = (weight * main_rows).astype(BF16).astype(F32)
        main_rows = main_rows.reshape(height // 2, 2, across, channels)
        last_row = bottom[2 + t, 0].astype(F32) + total[body_rows:]
        last_row = (weight * last_row * bottom_ok).astype(BF16).astype(F32)
        for part_at in range(lane_parts):
            lanes = slice(part_at * 128, (part_at + 1) * 128)
            mixed_all[part_at, t, 0 : height // 2] = main_rows[..., lanes]
            mixed_all[part_at, t, height // 2, 0] = last_row[:, lanes]

    half_rows, half_across = height // 2, across // 2
    points = frames * half_rows * half_across
    reduced = None
    for dr in range(3):
        rows_at, parity = (1 if dr == 2 else 0), dr % 2

        def every_second(first):
            columns = pl.ds(first, half_across, 2)
            return jnp.concatenate(
                [
                    mixed_all[at, :, rows_at : rows_at + half_rows, parity, columns, :].reshape(
                        points, 128
                    )
                    for at in range(lane_parts)
                ],
                axis=-1,
            )

        even, odd = every_second(0), every_second(1)
        column = lax.broadcasted_iota(jnp.int32, even.shape, 0) % half_across
        following = jnp.where(column == half_across - 1, 0.0, pltpu.roll(even, points - 1, 0))
        lhs = jnp.concatenate([even, odd, following], axis=-1).astype(BF16)
        tap = taps_conv + dr * 3
        rhs = w_all[tap : tap + 3].reshape(3 * channels, channels)
        product = jnp.dot(lhs, rhs, preferred_element_type=F32)
        reduced = product if reduced is None else reduced + product
    out[...] = reduced.astype(BF16)


def main_call(place, block, params, feat, prev, edge, swap, pieces):
    frames, height, across, channels = feat.shape
    taps = pieces[0].shape[0]
    points = frames * (height // 2) * (across // 2)
    vmem = pl.BlockSpec(memory_space=pltpu.VMEM)
    return pl.pallas_call(
        main_kernel,
        out_shape=jax.ShapeDtypeStruct((points, channels), BF16),
        in_specs=[pl.BlockSpec(memory_space=pltpu.SMEM)]
        + [vmem] * 11,
        out_specs=vmem,
        scratch_shapes=[
            pltpu.VMEM((taps, channels, channels), BF16),
            pltpu.VMEM((frames + 3, height + 3, across, 3 * channels), BF16),
            pltpu.VMEM((channels // 128, frames, height // 2 + 1, 2, across, 128), F32),
            pltpu.VMEM((frames + 2, 1, across, channels), BF16),
            pltpu.VMEM((frames + 2, 2, across, channels), BF16),
            pltpu.SemaphoreType.DMA((8,)),
        ],
        compiler_params=pltpu.CompilerParams(vmem_limit_bytes=24 << 20),
        name="norm_conv_down",
    )(place, block, params, feat, prev, edge, swap, *pieces)


def body(features, clip_ids, frame_valid, norm_gain, norm_bias, conv_weight, down_weight):
    frames, height, across, channels = features.shape
    slice_in = conv_weight.shape[3]
    place = jnp.stack([lax.axis_index("rows"), lax.axis_index("tm")]).astype(jnp.int32)

    bands, times = lax.axis_size("rows"), lax.axis_size("tm")

    plain = jnp.concatenate(
        [
            conv_weight.reshape(27, slice_in, channels),
            down_weight.reshape(9, slice_in, channels),
        ],
        axis=0,
    )
    near = ring_move(plain, "rows", 0)
    table, params, feat, tail = pack_call(
        clip_ids,
        frame_valid,
        features,
        norm_gain.reshape(1, channels),
        norm_bias.reshape(1, channels),
    )
    prev = shifted(tail, "tm", 1)
    near_cross = ring_move(plain, "rows", 1)

    half = BLOCK // 2
    pairs = [(at, at + (BLOCK if at % BLOCK >= half else -BLOCK)) for at in range(times)]
    sent = lax.ppermute(table, "tm", [pair for pair in pairs if 0 <= pair[1] < times])
    row = lax.broadcasted_iota(jnp.int32, table.shape, 0)
    rows = jnp.where(row < frames, table, sent)
    near, rows = lax.optimization_barrier((near, rows))
    far = ring_move(near, "rows", 0)
    size = BLOCK * bands
    groups = [[first + at for at in range(size)] for first in range(0, bands * times, size)]
    block = lax.all_to_all(
        jnp.broadcast_to(rows[None], (size, *rows.shape)),
        ("tm", "rows"),
        0,
        0,
        axis_index_groups=groups,
        tiled=True,
    ).reshape(BLOCK, bands, *rows.shape)

    prev, near_cross, far, block = lax.optimization_barrier((prev, near_cross, far, block))
    swap, edge = swap_call(place, feat, prev, plain, near, near_cross)
    swap = swapped(swap, "rows", 1)
    edge = ring_move(edge, "rows", 1)
    pieces = [plain, near, near_cross, far, swapped(far, "rows", 1)]

    out = main_call(place, block, params, feat, prev, edge, swap, pieces)
    return out.reshape(frames, height // 2, across // 2, channels)


def solution(mesh):
    return jax.shard_map(
        body,
        mesh=mesh,
        in_specs=(
            P("tm", "rows", None, None),
            P("tm"),
            P("tm"),
            P(),
            P(),
            P(None, None, None, "rows", None),
            P(None, None, "rows", None),
        ),
        out_specs=P("tm", "rows", None, None),
        check_vma=False,
    )
```

```python
import jax
import jax.numpy as jnp
from jax import lax
from jax.experimental import pallas as pl
from jax.experimental.pallas import tpu as pltpu
from jax.sharding import PartitionSpec as P

GROUPS = 32
ID_LANE = 64
VALID_LANE = 65
BLOCK = 4
F32 = jnp.float32
BF16 = jnp.bfloat16


def shifted(value, axis, steps):
    count = lax.axis_size(axis)
    first, last = (max(0, -steps), min(count, count - steps))
    return lax.ppermute(value, axis, [(source, source + steps) for source in range(first, last)])


def swapped(value, axis, bits):
    return lax.ppermute(value, axis, [(i, i ^ bits) for i in range(lax.axis_size(axis))])


def ring_move(value, axis, cross):
    chips = lax.axis_size(axis) // 2
    pairs = []
    for chip in range(chips):
        for core in range(2):
            source_chip = (chip + (-1 if core == 0 else 1)) % chips
            pairs.append((2 * source_chip + (core ^ cross), 2 * chip + core))
    return lax.ppermute(value, axis, pairs)


def group_lanes(channels, first):
    lane = lax.broadcasted_iota(jnp.int32, (channels, 128), 1)
    group = lax.broadcasted_iota(jnp.int32, (channels, 128), 0) // (channels // GROUPS) + first
    return (lane == group).astype(F32)


def exact_dot(lhs, rhs):
    return lax.dot_general(
        lhs,
        rhs,
        (((1,), (0,)), ((), ())),
        precision=lax.Precision.HIGHEST,
        preferred_element_type=F32,
    )


def pack_kernel(ids, valid, feat, gain, bias, table, params, kept):
    frames, height, across, channels = feat.shape
    kept[...] = feat[...]
    params[0:1, :] = gain[...]
    params[1:2, :] = bias[...]

    first, second = [], []
    for f in range(frames):
        block = feat[f].astype(F32).reshape(height * across, channels)
        first.append(jnp.sum(block, axis=0, keepdims=True))
        second.append(jnp.sum(block * block, axis=0, keepdims=True))
    rows = exact_dot(
        jnp.concatenate(first + first, axis=0), group_lanes(channels, 0)
    ) + exact_dot(jnp.concatenate(second + second, axis=0), group_lanes(channels, GROUPS))
    lane = lax.broadcasted_iota(jnp.int32, (1, 128), 1)
    for at in range(2 * frames):
        weight = valid[at % frames].astype(F32)
        row = rows[at : at + 1, :] * weight
        row = jnp.where(lane == ID_LANE, ids[at % frames].astype(F32) + 1.0, row)
        table[at : at + 1, :] = jnp.where(lane == VALID_LANE, weight, row)


def pack_call(clip_ids, frame_valid, features, gain, bias):
    frames, channels = features.shape[0], features.shape[-1]
    vmem = pl.BlockSpec(memory_space=pltpu.VMEM)
    return pl.pallas_call(
        pack_kernel,
        out_shape=(
            jax.ShapeDtypeStruct((2 * frames, 128), F32),
            jax.ShapeDtypeStruct((8, channels), F32),
            jax.ShapeDtypeStruct(features.shape, BF16),
        ),
        in_specs=[pl.BlockSpec(memory_space=pltpu.SMEM)] * 2 + [vmem] * 3,
        out_specs=(vmem,) * 3,
        compiler_params=pltpu.CompilerParams(vmem_limit_bytes=10 << 20),
        name="frame_sums",
    )(clip_ids, frame_valid, features, gain, bias)


def edges_kernel(place, feat, prev, chip_edge, core_edge):
    frames, height, across, channels = feat.shape
    for core in range(2):

        @pl.when(place[0] % 2 == core)
        def _(core=core):
            for target, side in ((chip_edge, core), (core_edge, 1 - core)):
                row = side * (height - 2)
                for source, first, count in ((prev, 0, 2), (feat, 2, frames)):
                    rows = source[:, row : row + 2].reshape(count, 2 * across, channels)
                    target[first : first + count] = rows


def edges_call(place, feat, prev):
    frames, height, across, channels = feat.shape
    vmem = pl.BlockSpec(memory_space=pltpu.VMEM)
    return pl.pallas_call(
        edges_kernel,
        out_shape=(jax.ShapeDtypeStruct((frames + 2, 2 * across, channels), BF16),) * 2,
        in_specs=[pl.BlockSpec(memory_space=pltpu.SMEM)] + [vmem] * 2,
        out_specs=(vmem,) * 2,
        compiler_params=pltpu.CompilerParams(vmem_limit_bytes=8 << 20),
        name="edge_rows",
    )(place, feat, prev)


def swap_kernel(core_edge, plain, near, swap):
    taps = plain.shape[0]
    for at, piece in enumerate((plain, near)):
        swap[at * taps : (at + 1) * taps] = piece[...]
    swap[2 * taps :] = core_edge[...]


def swap_call(core_edge, plain, near):
    rows = core_edge.shape[0]
    taps, slice_in, channels = plain.shape
    vmem = pl.BlockSpec(memory_space=pltpu.VMEM)
    return pl.pallas_call(
        swap_kernel,
        out_shape=jax.ShapeDtypeStruct((2 * taps + rows, slice_in, channels), BF16),
        in_specs=[vmem] * 3,
        out_specs=vmem,
        compiler_params=pltpu.CompilerParams(vmem_limit_bytes=8 << 20),
        name="swap_message",
    )(core_edge, plain, near)


def held_places(band):
    chip, core = band // 2, band % 2
    near_chip = (chip + 3 + 2 * core) % 4
    far_chip = (chip + 2) % 4
    return [band, 2 * near_chip + core, 2 * near_chip + 1 - core, 2 * far_chip + core]


def main_kernel(place, block, params, feat, prev, edge, *rest):
    swap, pieces = rest[0], rest[1:7]
    out, w_all, hcol, mixed_all, top, bottom, sems = rest[7:]
    frames, height, across, channels = feat.shape
    taps, slice_in = pieces[0].shape[:2]
    taps_conv = 27

    band = place[0]
    places = held_places(band) + held_places(band + 1 - 2 * (band % 2))
    sources = list(pieces[:4])
    sources += [swap.at[at * taps : (at + 1) * taps] for at in range(2)] + list(pieces[4:])
    copies = []
    for at in range(8):
        start = pl.multiple_of(places[at] * slice_in, slice_in)
        source, target = sources[at], w_all.at[:, pl.ds(start, slice_in), :]
        copies.append(pltpu.make_async_copy(source, target, sems.at[at]))
    for copy in copies:
        copy.start()

    for core in range(2):

        @pl.when(band % 2 == core)
        def _(core=core):
            swap_rows = swap[2 * taps :].reshape(frames + 2, 2, across, channels)
            edge_rows = edge[...].reshape(frames + 2, 2, across, channels)
            top[...] = (swap_rows if core else edge_rows)[:, 1:2]
            bottom[...] = edge_rows if core else swap_rows

    bands = block.shape[1]
    here = place[1] % BLOCK

    def lane_of(rows, at):
        lane = lax.broadcasted_iota(jnp.int32, rows.shape, 1)
        return jnp.sum(jnp.where(lane == at, rows, 0.0), axis=1, keepdims=True)

    own_rows = block[here, 0]
    own_ids = lane_of(own_rows, ID_LANE)
    own_valid = lane_of(own_rows, VALID_LANE)
    total = jnp.zeros((8, 128), F32)
    for device in range(BLOCK):
        table = block[device, 0]
        table_ids = lane_of(table, ID_LANE)
        for sender in range(1, bands):
            table = table + block[device, sender]
        for f in range(2 * frames):
            same = table_ids[f : f + 1] == own_ids
            total = total + jnp.where(same, table[f : f + 1, :], 0.0)
    group = channels // GROUPS
    count = lane_of(total, VALID_LANE) * float(height * across * group)
    safe = jnp.maximum(count, 1.0)
    both = total / safe
    lane_at = lax.broadcasted_iota(jnp.int32, (128, channels), 0)
    group_at = lax.broadcasted_iota(jnp.int32, (128, channels), 1) // group
    mean = exact_dot(both, (lane_at == group_at).astype(F32))
    square = exact_dot(both, (lane_at == group_at + GROUPS).astype(F32))
    variance = jnp.maximum(square - mean * mean, 0.0)
    half_scale = 0.5 * (lax.rsqrt(variance + 1e-05) * params[0:1, :])
    half_bias = 0.5 * params[1:2, :]

    before_own = block[jnp.maximum(here - 1, 0), 0][frames - 2 : frames]
    before_sent = block[BLOCK - 1, 0][2 * frames - 2 : 2 * frames]
    before_rows = jnp.where(here > 0, before_own, before_sent)
    before_ids = lane_of(before_rows, ID_LANE)
    before_valid = lane_of(before_rows, VALID_LANE)

    top_ok = (band > 0).astype(F32)
    bottom_ok = (band < bands - 1).astype(F32)

    def normalise(x, at, weight, j, first, inside=None):
        rows = x.shape[0]
        x = x.astype(F32).reshape(rows * across, channels)
        u = (x - mean[at : at + 1]) * half_scale[at : at + 1] + half_bias
        h = (u + u * jnp.tanh(u)) * weight
        if inside is not None:
            h = jnp.where(jnp.full(h.shape, inside) > 0.0, h, 0.0)
        column = lax.broadcasted_iota(jnp.int32, h.shape, 0) % across
        left = jnp.where(column == 0, 0.0, pltpu.roll(h, 1, 0))
        right = jnp.where(column == across - 1, 0.0, pltpu.roll(h, rows * across - 1, 0))
        shape = (rows, across, channels)
        hcol[j, pl.ds(first, rows), :, 0:channels] = left.astype(BF16).reshape(shape)
        hcol[j, pl.ds(first, rows), :, channels : 2 * channels] = h.astype(BF16).reshape(shape)
        hcol[j, pl.ds(first, rows), :, 2 * channels :] = right.astype(BF16).reshape(shape)

    rows_step = 4
    for j in range(frames + 2):
        at = max(j - 2, 0)
        if j < 2:
            weight = before_valid[j : j + 1]
            source, source_at = prev, j
        else:
            weight = own_valid[at : at + 1]
            source, source_at = feat, at
        normalise(top[j], at, weight, j, 0, top_ok)
        normalise(bottom[j], at, weight, j, height + 1, bottom_ok)

        @pl.loop(0, height // rows_step)
        def _(step):
            first = step * rows_step
            x = source[source_at, pl.ds(first, rows_step)]
            normalise(x, at, weight, j, first + 1)

    for copy in copies:
        copy.wait()

    out_rows = height + 1
    lane_parts = channels // 128
    hcol[frames + 2] = jnp.zeros(hcol.shape[1:], BF16)
    ids_all = [before_ids[f, 0] for f in range(2)] + [own_ids[f, 0] for f in range(frames)]
    for t in range(frames):
        total = None
        for dt in range(3):
            at = jnp.where(ids_all[t + dt] == ids_all[t + 2], t + dt, frames + 2)
            for dr in range(3):
                lhs = hcol[at, dr : dr + out_rows].reshape(out_rows * across, 3 * channels)
                tap = (dt * 3 + dr) * 3
                rhs = w_all[tap : tap + 3].reshape(3 * channels, channels)
                product = jnp.dot(lhs, rhs, preferred_element_type=F32)
                total = product if total is None else total + product
        weight = own_valid[t : t + 1]
        body_rows = height * across
        main_rows = feat[t].astype(F32).reshape(body_rows, channels) + total[:body_rows]
        main_rows = (weight * main_rows).astype(BF16).astype(F32)
        main_rows = main_rows.reshape(height // 2, 2, across, channels)
        last_row = bottom[2 + t, 0].astype(F32) + total[body_rows:]
        last_row = (weight * last_row * bottom_ok).astype(BF16).astype(F32)
        for part_at in range(lane_parts):
            lanes = slice(part_at * 128, (part_at + 1) * 128)
            mixed_all[part_at, t, 0 : height // 2] = main_rows[..., lanes]
            mixed_all[part_at, t, height // 2, 0] = last_row[:, lanes]

    half_rows, half_across = height // 2, across // 2
    points = frames * half_rows * half_across
    reduced = None
    for dr in range(3):
        rows_at, parity = (1 if dr == 2 else 0), dr % 2

        def every_second(first):
            columns = pl.ds(first, half_across, 2)
            return jnp.concatenate(
                [
                    mixed_all[at, :, rows_at : rows_at + half_rows, parity, columns, :].reshape(
                        points, 128
                    )
                    for at in range(lane_parts)
                ],
                axis=-1,
            )

        even, odd = every_second(0), every_second(1)
        column = lax.broadcasted_iota(jnp.int32, even.shape, 0) % half_across
        following = jnp.where(column == half_across - 1, 0.0, pltpu.roll(even, points - 1, 0))
        lhs = jnp.concatenate([even, odd, following], axis=-1).astype(BF16)
        tap = taps_conv + dr * 3
        rhs = w_all[tap : tap + 3].reshape(3 * channels, channels)
        product = jnp.dot(lhs, rhs, preferred_element_type=F32)
        reduced = product if reduced is None else reduced + product
    out[...] = reduced.astype(BF16)


def main_call(place, block, params, feat, prev, edge, swap, pieces):
    frames, height, across, channels = feat.shape
    taps = pieces[0].shape[0]
    points = frames * (height // 2) * (across // 2)
    vmem = pl.BlockSpec(memory_space=pltpu.VMEM)
    return pl.pallas_call(
        main_kernel,
        out_shape=jax.ShapeDtypeStruct((points, channels), BF16),
        in_specs=[pl.BlockSpec(memory_space=pltpu.SMEM)]
        + [vmem] * 12,
        out_specs=vmem,
        scratch_shapes=[
            pltpu.VMEM((taps, channels, channels), BF16),
            pltpu.VMEM((frames + 3, height + 3, across, 3 * channels), BF16),
            pltpu.VMEM((channels // 128, frames, height // 2 + 1, 2, across, 128), F32),
            pltpu.VMEM((frames + 2, 1, across, channels), BF16),
            pltpu.VMEM((frames + 2, 2, across, channels), BF16),
            pltpu.SemaphoreType.DMA((8,)),
        ],
        compiler_params=pltpu.CompilerParams(vmem_limit_bytes=24 << 20),
        name="norm_conv_down",
    )(place, block, params, feat, prev, edge, swap, *pieces)


def body(features, clip_ids, frame_valid, norm_gain, norm_bias, conv_weight, down_weight):
    frames, height, across, channels = features.shape
    slice_in = conv_weight.shape[3]
    place = jnp.stack([lax.axis_index("rows"), lax.axis_index("tm")]).astype(jnp.int32)

    bands, times = lax.axis_size("rows"), lax.axis_size("tm")

    prev = shifted(features[frames - 2 :], "tm", 1)
    plain = jnp.concatenate(
        [
            conv_weight.reshape(27, slice_in, channels),
            down_weight.reshape(9, slice_in, channels),
        ],
        axis=0,
    )
    near = ring_move(plain, "rows", 0)
    table, params, feat = pack_call(
        clip_ids,
        frame_valid,
        features,
        norm_gain.reshape(1, channels),
        norm_bias.reshape(1, channels),
    )
    near_cross = ring_move(plain, "rows", 1)

    half = BLOCK // 2
    pairs = [(at, at + (BLOCK if at % BLOCK >= half else -BLOCK)) for at in range(times)]
    sent = lax.ppermute(table, "tm", [pair for pair in pairs if 0 <= pair[1] < times])
    row = lax.broadcasted_iota(jnp.int32, table.shape, 0)
    rows = jnp.where(row < frames, table, sent)

    near, prev, rows = lax.optimization_barrier((near, prev, rows))
    chip_edge, core_edge = edges_call(place, feat, prev)
    edge = ring_move(chip_edge, "rows", 1)
    message = swap_call(core_edge, plain, near)
    near, near_cross, message, edge, rows = lax.optimization_barrier(
        (near, near_cross, message, edge, rows)
    )
    far = ring_move(near, "rows", 0)
    swap = swapped(message, "rows", 1)
    cross_swapped = swapped(near_cross, "rows", 1)
    size = BLOCK * bands
    groups = [[first + at for at in range(size)] for first in range(0, bands * times, size)]
    block = lax.all_to_all(
        jnp.broadcast_to(rows[None], (size, *rows.shape)),
        ("tm", "rows"),
        0,
        0,
        axis_index_groups=groups,
        tiled=True,
    ).reshape(BLOCK, bands, *rows.shape)

    far, block = lax.optimization_barrier((far, block))
    pieces = [plain, near, near_cross, far, cross_swapped, swapped(far, "rows", 1)]

    out = main_call(place, block, params, feat, prev, edge, swap, pieces)
    return out.reshape(frames, height // 2, across // 2, channels)


def solution(mesh):
    return jax.shard_map(
        body,
        mesh=mesh,
        in_specs=(
            P("tm", "rows", None, None),
            P("tm"),
            P("tm"),
            P(),
            P(),
            P(None, None, None, "rows", None),
            P(None, None, "rows", None),
        ),
        out_specs=P("tm", "rows", None, None),
        check_vma=False,
    )
```

```python
import jax
import jax.numpy as jnp
from jax import lax
from jax.experimental import pallas as pl
from jax.experimental.pallas import tpu as pltpu
from jax.sharding import PartitionSpec as P

GROUPS = 32
ID_LANE = 64
VALID_LANE = 65
BLOCK = 4
F32 = jnp.float32
BF16 = jnp.bfloat16


def shifted(value, axis, steps):
    count = lax.axis_size(axis)
    first, last = (max(0, -steps), min(count, count - steps))
    return lax.ppermute(value, axis, [(source, source + steps) for source in range(first, last)])


def swapped(value, axis, bits):
    return lax.ppermute(value, axis, [(i, i ^ bits) for i in range(lax.axis_size(axis))])


def ring_move(value, axis, cross):
    chips = lax.axis_size(axis) // 2
    pairs = []
    for chip in range(chips):
        for core in range(2):
            source_chip = (chip + (-1 if core == 0 else 1)) % chips
            pairs.append((2 * source_chip + (core ^ cross), 2 * chip + core))
    return lax.ppermute(value, axis, pairs)


def group_lanes(channels, first):
    lane = lax.broadcasted_iota(jnp.int32, (channels, 128), 1)
    group = lax.broadcasted_iota(jnp.int32, (channels, 128), 0) // (channels // GROUPS) + first
    return (lane == group).astype(F32)


def exact_dot(lhs, rhs):
    return lax.dot_general(
        lhs,
        rhs,
        (((1,), (0,)), ((), ())),
        precision=lax.Precision.HIGHEST,
        preferred_element_type=F32,
    )


def pack_kernel(ids, valid, feat, gain, bias, table, params, kept):
    frames, height, across, channels = feat.shape
    kept[...] = feat[...]
    params[0:1, :] = gain[...]
    params[1:2, :] = bias[...]

    first, second = [], []
    for f in range(frames):
        block = feat[f].astype(F32).reshape(height * across, channels)
        first.append(jnp.sum(block, axis=0, keepdims=True))
        second.append(jnp.sum(block * block, axis=0, keepdims=True))
    rows = exact_dot(
        jnp.concatenate(first + first, axis=0), group_lanes(channels, 0)
    ) + exact_dot(jnp.concatenate(second + second, axis=0), group_lanes(channels, GROUPS))
    lane = lax.broadcasted_iota(jnp.int32, (1, 128), 1)
    for at in range(2 * frames):
        weight = valid[at % frames].astype(F32)
        row = rows[at : at + 1, :] * weight
        row = jnp.where(lane == ID_LANE, ids[at % frames].astype(F32) + 1.0, row)
        table[at : at + 1, :] = jnp.where(lane == VALID_LANE, weight, row)


def pack_call(clip_ids, frame_valid, features, gain, bias):
    frames, channels = features.shape[0], features.shape[-1]
    vmem = pl.BlockSpec(memory_space=pltpu.VMEM)
    return pl.pallas_call(
        pack_kernel,
        out_shape=(
            jax.ShapeDtypeStruct((2 * frames, 128), F32),
            jax.ShapeDtypeStruct((8, channels), F32),
            jax.ShapeDtypeStruct(features.shape, BF16),
        ),
        in_specs=[pl.BlockSpec(memory_space=pltpu.SMEM)] * 2 + [vmem] * 3,
        out_specs=(vmem,) * 3,
        compiler_params=pltpu.CompilerParams(vmem_limit_bytes=10 << 20),
        name="frame_sums",
    )(clip_ids, frame_valid, features, gain, bias)


def edges_kernel(place, feat, prev, plain, swap, edge):
    frames, height, across, channels = feat.shape
    taps, slice_in, _ = plain.shape
    swap[0:taps] = plain[...]
    for core in range(2):

        @pl.when(place[0] % 2 == core)
        def _(core=core):
            for source, first, count in ((prev, 0, 2), (feat, 2, frames)):
                first_rows = source[:, 0:2].reshape(count, slice_in, channels)
                last_rows = source[:, height - 2 :].reshape(count, slice_in, channels)
                edge[first : first + count] = last_rows if core else first_rows
                swap[taps + first : taps + first + count] = first_rows if core else last_rows


def edges_call(place, feat, prev, plain):
    frames, height, across, channels = feat.shape
    taps, slice_in, _ = plain.shape
    vmem = pl.BlockSpec(memory_space=pltpu.VMEM)
    return pl.pallas_call(
        edges_kernel,
        out_shape=(
            jax.ShapeDtypeStruct((taps + frames + 2, slice_in, channels), BF16),
            jax.ShapeDtypeStruct((frames + 2, slice_in, channels), BF16),
        ),
        in_specs=[pl.BlockSpec(memory_space=pltpu.SMEM)] + [vmem] * 3,
        out_specs=(vmem,) * 2,
        compiler_params=pltpu.CompilerParams(vmem_limit_bytes=8 << 20),
        name="edge_rows",
    )(place, feat, prev, plain)


def held_places(band):
    chip, core = band // 2, band % 2
    near_chip = (chip + 3 + 2 * core) % 4
    far_chip = (chip + 2) % 4
    return [band, 2 * near_chip + core, 2 * near_chip + 1 - core, 2 * far_chip + core]


def main_kernel(place, block, params, feat, prev, edge, *rest):
    pieces, (out, w_all, hcol, mixed_all, top, bottom, sems) = rest[:8], rest[8:]
    frames, height, across, channels = feat.shape
    taps, slice_in = pieces[0].shape[:2]
    taps_conv = 27

    band = place[0]
    places = held_places(band) + held_places(band + 1 - 2 * (band % 2))
    copies = []
    for at in range(8):
        start = pl.multiple_of(places[at] * slice_in, slice_in)
        source, target = pieces[at].at[0:taps], w_all.at[:, pl.ds(start, slice_in), :]
        copies.append(pltpu.make_async_copy(source, target, sems.at[at]))
    for copy in copies:
        copy.start()

    swap = pieces[4]
    for core in range(2):

        @pl.when(band % 2 == core)
        def _(core=core):
            swap_rows = swap[taps:].reshape(frames + 2, 2, across, channels)
            edge_rows = edge[...].reshape(frames + 2, 2, across, channels)
            top[...] = (swap_rows if core else edge_rows)[:, 1:2]
            bottom[...] = edge_rows if core else swap_rows

    bands = block.shape[1]
    here = place[1] % BLOCK

    def lane_of(rows, at):
        lane = lax.broadcasted_iota(jnp.int32, rows.shape, 1)
        return jnp.sum(jnp.where(lane == at, rows, 0.0), axis=1, keepdims=True)

    own_rows = block[here, 0]
    own_ids = lane_of(own_rows, ID_LANE)
    own_valid = lane_of(own_rows, VALID_LANE)
    total = jnp.zeros((8, 128), F32)
    for device in range(BLOCK):
        table = block[device, 0]
        table_ids = lane_of(table, ID_LANE)
        for sender in range(1, bands):
            table = table + block[device, sender]
        for f in range(2 * frames):
            same = table_ids[f : f + 1] == own_ids
            total = total + jnp.where(same, table[f : f + 1, :], 0.0)
    group = channels // GROUPS
    count = lane_of(total, VALID_LANE) * float(height * across * group)
    safe = jnp.maximum(count, 1.0)
    both = total / safe
    lane_at = lax.broadcasted_iota(jnp.int32, (128, channels), 0)
    group_at = lax.broadcasted_iota(jnp.int32, (128, channels), 1) // group
    mean = exact_dot(both, (lane_at == group_at).astype(F32))
    square = exact_dot(both, (lane_at == group_at + GROUPS).astype(F32))
    variance = jnp.maximum(square - mean * mean, 0.0)
    half_scale = 0.5 * (lax.rsqrt(variance + 1e-05) * params[0:1, :])
    half_bias = 0.5 * params[1:2, :]

    before_own = block[jnp.maximum(here - 1, 0), 0][frames - 2 : frames]
    before_sent = block[BLOCK - 1, 0][2 * frames - 2 : 2 * frames]
    before_rows = jnp.where(here > 0, before_own, before_sent)
    before_ids = lane_of(before_rows, ID_LANE)
    before_valid = lane_of(before_rows, VALID_LANE)

    top_ok = (band > 0).astype(F32)
    bottom_ok = (band < bands - 1).astype(F32)

    def normalise(x, at, weight, j, first, inside=None):
        rows = x.shape[0]
        x = x.astype(F32).reshape(rows * across, channels)
        u = (x - mean[at : at + 1]) * half_scale[at : at + 1] + half_bias
        h = (u + u * jnp.tanh(u)) * weight
        if inside is not None:
            h = jnp.where(jnp.full(h.shape, inside) > 0.0, h, 0.0)
        column = lax.broadcasted_iota(jnp.int32, h.shape, 0) % across
        left = jnp.where(column == 0, 0.0, pltpu.roll(h, 1, 0))
        right = jnp.where(column == across - 1, 0.0, pltpu.roll(h, rows * across - 1, 0))
        shape = (rows, across, channels)
        hcol[j, pl.ds(first, rows), :, 0:channels] = left.astype(BF16).reshape(shape)
        hcol[j, pl.ds(first, rows), :, channels : 2 * channels] = h.astype(BF16).reshape(shape)
        hcol[j, pl.ds(first, rows), :, 2 * channels :] = right.astype(BF16).reshape(shape)

    rows_step = 4
    for j in range(frames + 2):
        at = max(j - 2, 0)
        if j < 2:
            weight = before_valid[j : j + 1]
            source, source_at = prev, j
        else:
            weight = own_valid[at : at + 1]
            source, source_at = feat, at
        normalise(top[j], at, weight, j, 0, top_ok)
        normalise(bottom[j], at, weight, j, height + 1, bottom_ok)

        @pl.loop(0, height // rows_step)
        def _(step):
            first = step * rows_step
            x = source[source_at, pl.ds(first, rows_step)]
            normalise(x, at, weight, j, first + 1)

    for copy in copies:
        copy.wait()

    out_rows = height + 1
    lane_parts = channels // 128
    ids_all = [before_ids[f : f + 1] for f in range(2)]
    ids_all = ids_all + [own_ids[f : f + 1] for f in range(frames)]
    for t in range(frames):
        total = None
        for dt in (2, 1, 0):
            part = None
            for dr in range(3):
                lhs = hcol[t + dt, dr : dr + out_rows].reshape(out_rows * across, 3 * channels)
                tap = (dt * 3 + dr) * 3
                rhs = w_all[tap : tap + 3].reshape(3 * channels, channels)
                product = jnp.dot(lhs, rhs, preferred_element_type=F32)
                part = product if part is None else part + product
            if dt == 2:
                total = part
            else:
                total = total + jnp.where(ids_all[t + dt] == ids_all[t + 2], part, 0.0)
        weight = own_valid[t : t + 1]
        body_rows = height * across
        main_rows = feat[t].astype(F32).reshape(body_rows, channels) + total[:body_rows]
        main_rows = (weight * main_rows).astype(BF16).astype(F32)
        main_rows = main_rows.reshape(height // 2, 2, across, channels)
        last_row = bottom[2 + t, 0].astype(F32) + total[body_rows:]
        last_row = (weight * last_row * bottom_ok).astype(BF16).astype(F32)
        for part_at in range(lane_parts):
            lanes = slice(part_at * 128, (part_at + 1) * 128)
            mixed_all[part_at, t, 0 : height // 2] = main_rows[..., lanes]
            mixed_all[part_at, t, height // 2, 0] = last_row[:, lanes]

    half_rows, half_across = height // 2, across // 2
    points = frames * half_rows * half_across
    reduced = None
    for dr in range(3):
        rows_at, parity = (1 if dr == 2 else 0), dr % 2

        def every_second(first):
            columns = pl.ds(first, half_across, 2)
            return jnp.concatenate(
                [
                    mixed_all[at, :, rows_at : rows_at + half_rows, parity, columns, :].reshape(
                        points, 128
                    )
                    for at in range(lane_parts)
                ],
                axis=-1,
            )

        even, odd = every_second(0), every_second(1)
        column = lax.broadcasted_iota(jnp.int32, even.shape, 0) % half_across
        following = jnp.where(column == half_across - 1, 0.0, pltpu.roll(even, points - 1, 0))
        lhs = jnp.concatenate([even, odd, following], axis=-1).astype(BF16)
        tap = taps_conv + dr * 3
        rhs = w_all[tap : tap + 3].reshape(3 * channels, channels)
        product = jnp.dot(lhs, rhs, preferred_element_type=F32)
        reduced = product if reduced is None else reduced + product
    out[...] = reduced.astype(BF16)


def main_call(place, block, params, feat, prev, edge, pieces):
    frames, height, across, channels = feat.shape
    taps = pieces[0].shape[0]
    points = frames * (height // 2) * (across // 2)
    vmem = pl.BlockSpec(memory_space=pltpu.VMEM)
    return pl.pallas_call(
        main_kernel,
        out_shape=jax.ShapeDtypeStruct((points, channels), BF16),
        in_specs=[pl.BlockSpec(memory_space=pltpu.SMEM)]
        + [vmem] * 13,
        out_specs=vmem,
        scratch_shapes=[
            pltpu.VMEM((taps, channels, channels), BF16),
            pltpu.VMEM((frames + 2, height + 3, across, 3 * channels), BF16),
            pltpu.VMEM((channels // 128, frames, height // 2 + 1, 2, across, 128), F32),
            pltpu.VMEM((frames + 2, 1, across, channels), BF16),
            pltpu.VMEM((frames + 2, 2, across, channels), BF16),
            pltpu.SemaphoreType.DMA((8,)),
        ],
        compiler_params=pltpu.CompilerParams(vmem_limit_bytes=24 << 20),
        name="norm_conv_down",
    )(place, block, params, feat, prev, edge, *pieces)


def body(features, clip_ids, frame_valid, norm_gain, norm_bias, conv_weight, down_weight):
    frames, height, across, channels = features.shape
    slice_in = conv_weight.shape[3]
    place = jnp.stack([lax.axis_index("rows"), lax.axis_index("tm")]).astype(jnp.int32)

    bands, times = lax.axis_size("rows"), lax.axis_size("tm")

    prev = shifted(features[frames - 2 :], "tm", 1)
    plain = jnp.concatenate(
        [
            conv_weight.reshape(27, slice_in, channels),
            down_weight.reshape(9, slice_in, channels),
        ],
        axis=0,
    )
    near = ring_move(plain, "rows", 0)
    table, params, feat = pack_call(
        clip_ids,
        frame_valid,
        features,
        norm_gain.reshape(1, channels),
        norm_bias.reshape(1, channels),
    )
    near_cross = ring_move(plain, "rows", 1)

    half = BLOCK // 2
    pairs = [(at, at + (BLOCK if at % BLOCK >= half else -BLOCK)) for at in range(times)]
    sent = lax.ppermute(table, "tm", [pair for pair in pairs if 0 <= pair[1] < times])
    row = lax.broadcasted_iota(jnp.int32, table.shape, 0)
    rows = jnp.where(row < frames, table, sent)

    near, prev, rows = lax.optimization_barrier((near, prev, rows))
    far = ring_move(near, "rows", 0)
    near_swapped = swapped(near, "rows", 1)
    swap, edge = edges_call(place, feat, prev, plain)
    edge = ring_move(edge, "rows", 1)
    swap, edge = lax.optimization_barrier((swap, edge))
    other = swapped(swap, "rows", 1)
    near_cross, rows = lax.optimization_barrier((near_cross, rows))
    cross_swapped = swapped(near_cross, "rows", 1)

    size = BLOCK * bands
    groups = [[first + at for at in range(size)] for first in range(0, bands * times, size)]
    block = lax.all_to_all(
        jnp.broadcast_to(rows[None], (size, *rows.shape)),
        ("tm", "rows"),
        0,
        0,
        axis_index_groups=groups,
        tiled=True,
    ).reshape(BLOCK, bands, *rows.shape)

    far, block = lax.optimization_barrier((far, block))
    far_swapped = swapped(far, "rows", 1)
    pieces = [plain, near, near_cross, far, other, near_swapped, cross_swapped, far_swapped]

    out = main_call(place, block, params, feat, prev, edge, pieces)
    return out.reshape(frames, height // 2, across // 2, channels)


def solution(mesh):
    return jax.shard_map(
        body,
        mesh=mesh,
        in_specs=(
            P("tm", "rows", None, None),
            P("tm"),
            P("tm"),
            P(),
            P(),
            P(None, None, None, "rows", None),
            P(None, None, "rows", None),
        ),
        out_specs=P("tm", "rows", None, None),
        check_vma=False,
    )
```

```python
import jax
import jax.numpy as jnp
from jax import lax
from jax.experimental import pallas as pl
from jax.experimental.pallas import tpu as pltpu
from jax.sharding import PartitionSpec as P

GROUPS = 32
ID_LANE = 64
VALID_LANE = 65
BLOCK = 4
F32 = jnp.float32
BF16 = jnp.bfloat16


def shifted(value, axis, steps):
    count = lax.axis_size(axis)
    first, last = (max(0, -steps), min(count, count - steps))
    return lax.ppermute(value, axis, [(source, source + steps) for source in range(first, last)])


def swapped(value, axis, bits):
    return lax.ppermute(value, axis, [(i, i ^ bits) for i in range(lax.axis_size(axis))])


def ring_move(value, axis, cross):
    chips = lax.axis_size(axis) // 2
    pairs = []
    for chip in range(chips):
        for core in range(2):
            source_chip = (chip + (-1 if core == 0 else 1)) % chips
            pairs.append((2 * source_chip + (core ^ cross), 2 * chip + core))
    return lax.ppermute(value, axis, pairs)


def group_lanes(channels, first):
    lane = lax.broadcasted_iota(jnp.int32, (channels, 128), 1)
    group = lax.broadcasted_iota(jnp.int32, (channels, 128), 0) // (channels // GROUPS) + first
    return (lane == group).astype(F32)


def exact_dot(lhs, rhs):
    return lax.dot_general(
        lhs,
        rhs,
        (((1,), (0,)), ((), ())),
        precision=lax.Precision.HIGHEST,
        preferred_element_type=F32,
    )


def pack_kernel(ids, valid, feat, gain, bias, table, params, kept):
    frames, height, across, channels = feat.shape
    kept[...] = feat[...]
    params[0:1, :] = gain[...]
    params[1:2, :] = bias[...]

    first, second = [], []
    for f in range(frames):
        block = feat[f].astype(F32).reshape(height * across, channels)
        first.append(jnp.sum(block, axis=0, keepdims=True))
        second.append(jnp.sum(block * block, axis=0, keepdims=True))
    rows = exact_dot(
        jnp.concatenate(first + first, axis=0), group_lanes(channels, 0)
    ) + exact_dot(jnp.concatenate(second + second, axis=0), group_lanes(channels, GROUPS))
    lane = lax.broadcasted_iota(jnp.int32, (1, 128), 1)
    for at in range(2 * frames):
        weight = valid[at % frames].astype(F32)
        row = rows[at : at + 1, :] * weight
        row = jnp.where(lane == ID_LANE, ids[at % frames].astype(F32) + 1.0, row)
        table[at : at + 1, :] = jnp.where(lane == VALID_LANE, weight, row)


def pack_call(clip_ids, frame_valid, features, gain, bias):
    frames, channels = features.shape[0], features.shape[-1]
    vmem = pl.BlockSpec(memory_space=pltpu.VMEM)
    return pl.pallas_call(
        pack_kernel,
        out_shape=(
            jax.ShapeDtypeStruct((2 * frames, 128), F32),
            jax.ShapeDtypeStruct((8, channels), F32),
            jax.ShapeDtypeStruct(features.shape, BF16),
        ),
        in_specs=[pl.BlockSpec(memory_space=pltpu.SMEM)] * 2 + [vmem] * 3,
        out_specs=(vmem,) * 3,
        compiler_params=pltpu.CompilerParams(vmem_limit_bytes=10 << 20),
        name="frame_sums",
    )(clip_ids, frame_valid, features, gain, bias)


def edges_kernel(place, feat, prev, plain, swap, edge):
    frames, height, across, channels = feat.shape
    taps, slice_in, _ = plain.shape
    swap[0:taps] = plain[...]
    for core in range(2):

        @pl.when(place[0] % 2 == core)
        def _(core=core):
            for source, first, count in ((prev, 0, 2), (feat, 2, frames)):
                first_rows = source[:, 0:2].reshape(count, slice_in, channels)
                last_rows = source[:, height - 2 :].reshape(count, slice_in, channels)
                edge[first : first + count] = last_rows if core else first_rows
                swap[taps + first : taps + first + count] = first_rows if core else last_rows


def edges_call(place, feat, prev, plain):
    frames, height, across, channels = feat.shape
    taps, slice_in, _ = plain.shape
    vmem = pl.BlockSpec(memory_space=pltpu.VMEM)
    return pl.pallas_call(
        edges_kernel,
        out_shape=(
            jax.ShapeDtypeStruct((taps + frames + 2, slice_in, channels), BF16),
            jax.ShapeDtypeStruct((frames + 2, slice_in, channels), BF16),
        ),
        in_specs=[pl.BlockSpec(memory_space=pltpu.SMEM)] + [vmem] * 3,
        out_specs=(vmem,) * 2,
        compiler_params=pltpu.CompilerParams(vmem_limit_bytes=8 << 20),
        name="edge_rows",
    )(place, feat, prev, plain)


def held_places(band):
    chip, core = band // 2, band % 2
    near_chip = (chip + 3 + 2 * core) % 4
    far_chip = (chip + 2) % 4
    return [band, 2 * near_chip + core, 2 * near_chip + 1 - core, 2 * far_chip + core]


def main_kernel(place, block, params, feat, prev, edge, *rest):
    pieces, (out, w_all, hcol, mixed_all, top, bottom, sems) = rest[:8], rest[8:]
    frames, height, across, channels = feat.shape
    taps, slice_in = pieces[0].shape[:2]
    taps_conv = 27

    band = place[0]
    places = held_places(band) + held_places(band + 1 - 2 * (band % 2))
    copies = []
    for at in range(8):
        start = pl.multiple_of(places[at] * slice_in, slice_in)
        source, target = pieces[at].at[0:taps], w_all.at[:, pl.ds(start, slice_in), :]
        copies.append(pltpu.make_async_copy(source, target, sems.at[at]))
    for copy in copies:
        copy.start()

    swap = pieces[4]
    for core in range(2):

        @pl.when(band % 2 == core)
        def _(core=core):
            swap_rows = swap[taps:].reshape(frames + 2, 2, across, channels)
            edge_rows = edge[...].reshape(frames + 2, 2, across, channels)
            top[...] = (swap_rows if core else edge_rows)[:, 1:2]
            bottom[...] = edge_rows if core else swap_rows

    bands = block.shape[1]
    here = place[1] % BLOCK

    def lane_of(rows, at):
        lane = lax.broadcasted_iota(jnp.int32, rows.shape, 1)
        return jnp.sum(jnp.where(lane == at, rows, 0.0), axis=1, keepdims=True)

    own_rows = block[here, 0]
    own_ids = lane_of(own_rows, ID_LANE)
    own_valid = lane_of(own_rows, VALID_LANE)
    total = jnp.zeros((8, 128), F32)
    for device in range(BLOCK):
        table = block[device, 0]
        table_ids = lane_of(table, ID_LANE)
        for sender in range(1, bands):
            table = table + block[device, sender]
        for f in range(2 * frames):
            same = table_ids[f : f + 1] == own_ids
            total = total + jnp.where(same, table[f : f + 1, :], 0.0)
    group = channels // GROUPS
    count = lane_of(total, VALID_LANE) * float(height * across * group)
    safe = jnp.maximum(count, 1.0)
    both = total / safe
    lane_at = lax.broadcasted_iota(jnp.int32, (128, channels), 0)
    group_at = lax.broadcasted_iota(jnp.int32, (128, channels), 1) // group
    mean = exact_dot(both, (lane_at == group_at).astype(F32))
    square = exact_dot(both, (lane_at == group_at + GROUPS).astype(F32))
    variance = jnp.maximum(square - mean * mean, 0.0)
    half_scale = 0.5 * (lax.rsqrt(variance + 1e-05) * params[0:1, :])
    half_bias = 0.5 * params[1:2, :]

    before_own = block[jnp.maximum(here - 1, 0), 0][frames - 2 : frames]
    before_sent = block[BLOCK - 1, 0][2 * frames - 2 : 2 * frames]
    before_rows = jnp.where(here > 0, before_own, before_sent)
    before_ids = lane_of(before_rows, ID_LANE)
    before_valid = lane_of(before_rows, VALID_LANE)

    top_ok = (band > 0).astype(F32)
    bottom_ok = (band < bands - 1).astype(F32)

    def normalise(x, at, weight, j, first, inside=None):
        rows = x.shape[0]
        x = x.astype(F32).reshape(rows * across, channels)
        u = (x - mean[at : at + 1]) * half_scale[at : at + 1] + half_bias
        h = (u + u * jnp.tanh(u)) * weight
        if inside is not None:
            h = jnp.where(jnp.full(h.shape, inside) > 0.0, h, 0.0)
        column = lax.broadcasted_iota(jnp.int32, h.shape, 0) % across
        left = jnp.where(column == 0, 0.0, pltpu.roll(h, 1, 0))
        right = jnp.where(column == across - 1, 0.0, pltpu.roll(h, rows * across - 1, 0))
        shape = (rows, across, channels)
        hcol[j, pl.ds(first, rows), :, 0:channels] = left.astype(BF16).reshape(shape)
        hcol[j, pl.ds(first, rows), :, channels : 2 * channels] = h.astype(BF16).reshape(shape)
        hcol[j, pl.ds(first, rows), :, 2 * channels :] = right.astype(BF16).reshape(shape)

    rows_step = 4
    for j in range(frames + 2):
        at = max(j - 2, 0)
        if j < 2:
            weight = before_valid[j : j + 1]
            source, source_at = prev, j
        else:
            weight = own_valid[at : at + 1]
            source, source_at = feat, at
        normalise(top[j], at, weight, j, 0, top_ok)
        normalise(bottom[j], at, weight, j, height + 1, bottom_ok)

        @pl.loop(0, height // rows_step)
        def _(step):
            first = step * rows_step
            x = source[source_at, pl.ds(first, rows_step)]
            normalise(x, at, weight, j, first + 1)

    for copy in copies:
        copy.wait()

    out_rows = height + 1
    lane_parts = channels // 128
    hcol[frames + 2] = jnp.zeros(hcol.shape[1:], BF16)
    ids_all = [before_ids[f, 0] for f in range(2)] + [own_ids[f, 0] for f in range(frames)]
    for t in range(frames):
        total = None
        for dt in range(3):
            at = jnp.where(ids_all[t + dt] == ids_all[t + 2], t + dt, frames + 2)
            for dr in range(3):
                lhs = hcol[at, dr : dr + out_rows].reshape(out_rows * across, 3 * channels)
                tap = (dt * 3 + dr) * 3
                rhs = w_all[tap : tap + 3].reshape(3 * channels, channels)
                product = jnp.dot(lhs, rhs, preferred_element_type=F32)
                total = product if total is None else total + product
        weight = own_valid[t : t + 1]
        body_rows = height * across
        main_rows = feat[t].astype(F32).reshape(body_rows, channels) + total[:body_rows]
        main_rows = (weight * main_rows).astype(BF16).astype(F32)
        main_rows = main_rows.reshape(height // 2, 2, across, channels)
        last_row = bottom[2 + t, 0].astype(F32) + total[body_rows:]
        last_row = (weight * last_row * bottom_ok).astype(BF16).astype(F32)
        for part_at in range(lane_parts):
            lanes = slice(part_at * 128, (part_at + 1) * 128)
            mixed_all[part_at, t, 0 : height // 2] = main_rows[..., lanes]
            mixed_all[part_at, t, height // 2, 0] = last_row[:, lanes]

    half_rows, half_across = height // 2, across // 2
    points = frames * half_rows * half_across
    reduced = None
    for dr in range(3):
        rows_at, parity = (1 if dr == 2 else 0), dr % 2

        def every_second(first):
            columns = pl.ds(first, half_across, 2)
            return jnp.concatenate(
                [
                    mixed_all[at, :, rows_at : rows_at + half_rows, parity, columns, :].reshape(
                        points, 128
                    )
                    for at in range(lane_parts)
                ],
                axis=-1,
            )

        even, odd = every_second(0), every_second(1)
        column = lax.broadcasted_iota(jnp.int32, even.shape, 0) % half_across
        following = jnp.where(column == half_across - 1, 0.0, pltpu.roll(even, points - 1, 0))
        lhs = jnp.concatenate([even, odd, following], axis=-1).astype(BF16)
        tap = taps_conv + dr * 3
        rhs = w_all[tap : tap + 3].reshape(3 * channels, channels)
        product = jnp.dot(lhs, rhs, preferred_element_type=F32)
        reduced = product if reduced is None else reduced + product
    out[...] = reduced.astype(BF16)


def main_call(place, block, params, feat, prev, edge, pieces):
    frames, height, across, channels = feat.shape
    taps = pieces[0].shape[0]
    points = frames * (height // 2) * (across // 2)
    vmem = pl.BlockSpec(memory_space=pltpu.VMEM)
    return pl.pallas_call(
        main_kernel,
        out_shape=jax.ShapeDtypeStruct((points, channels), BF16),
        in_specs=[pl.BlockSpec(memory_space=pltpu.SMEM)]
        + [vmem] * 13,
        out_specs=vmem,
        scratch_shapes=[
            pltpu.VMEM((taps, channels, channels), BF16),
            pltpu.VMEM((frames + 3, height + 3, across, 3 * channels), BF16),
            pltpu.VMEM((channels // 128, frames, height // 2 + 1, 2, across, 128), F32),
            pltpu.VMEM((frames + 2, 1, across, channels), BF16),
            pltpu.VMEM((frames + 2, 2, across, channels), BF16),
            pltpu.SemaphoreType.DMA((8,)),
        ],
        compiler_params=pltpu.CompilerParams(vmem_limit_bytes=20 << 20),
        name="norm_conv_down",
    )(place, block, params, feat, prev, edge, *pieces)


def body(features, clip_ids, frame_valid, norm_gain, norm_bias, conv_weight, down_weight):
    frames, height, across, channels = features.shape
    slice_in = conv_weight.shape[3]
    place = jnp.stack([lax.axis_index("rows"), lax.axis_index("tm")]).astype(jnp.int32)

    bands, times = lax.axis_size("rows"), lax.axis_size("tm")

    prev = shifted(features[frames - 2 :], "tm", 1)
    plain = jnp.concatenate(
        [
            conv_weight.reshape(27, slice_in, channels),
            down_weight.reshape(9, slice_in, channels),
        ],
        axis=0,
    )
    near = ring_move(plain, "rows", 0)
    table, params, feat = pack_call(
        clip_ids,
        frame_valid,
        features,
        norm_gain.reshape(1, channels),
        norm_bias.reshape(1, channels),
    )
    near_cross = ring_move(plain, "rows", 1)

    half = BLOCK // 2
    pairs = [(at, at + (BLOCK if at % BLOCK >= half else -BLOCK)) for at in range(times)]
    sent = lax.ppermute(table, "tm", [pair for pair in pairs if 0 <= pair[1] < times])
    row = lax.broadcasted_iota(jnp.int32, table.shape, 0)
    rows = jnp.where(row < frames, table, sent)

    near, prev, rows = lax.optimization_barrier((near, prev, rows))
    far = ring_move(near, "rows", 0)
    near_swapped = swapped(near, "rows", 1)
    swap, edge = edges_call(place, feat, prev, plain)
    edge = ring_move(edge, "rows", 1)
    swap, edge = lax.optimization_barrier((swap, edge))
    other = swapped(swap, "rows", 1)
    near_cross, rows = lax.optimization_barrier((near_cross, rows))
    cross_swapped = swapped(near_cross, "rows", 1)

    size = BLOCK * bands
    groups = [[first + at for at in range(size)] for first in range(0, bands * times, size)]
    block = lax.all_to_all(
        jnp.broadcast_to(rows[None], (size, *rows.shape)),
        ("tm", "rows"),
        0,
        0,
        axis_index_groups=groups,
        tiled=True,
    ).reshape(BLOCK, bands, *rows.shape)

    far, block = lax.optimization_barrier((far, block))
    far_swapped = swapped(far, "rows", 1)
    pieces = [plain, near, near_cross, far, other, near_swapped, cross_swapped, far_swapped]

    out = main_call(place, block, params, feat, prev, edge, pieces)
    return out.reshape(frames, height // 2, across // 2, channels)


def solution(mesh):
    return jax.shard_map(
        body,
        mesh=mesh,
        in_specs=(
            P("tm", "rows", None, None),
            P("tm"),
            P("tm"),
            P(),
            P(),
            P(None, None, None, "rows", None),
            P(None, None, "rows", None),
        ),
        out_specs=P("tm", "rows", None, None),
        check_vma=False,
    )
```
